128 devices in a mesh: seq: 16 (over x, z), mp: 8 (over y, core).
Axes of the slice: x: 4, y: 4, z: 4, core: 2. Of those that a mesh axis runs over, the one named last changes fastest.
Arguments:
- context: bfloat16 [16, 256, 8192], P(None, 'mp', 'seq'), may hold values from -6 to 6
- blocks: bfloat16 [8, 8, 34, 128, 128], P('mp'), may hold values from -0.09375 to 0.09375
- row_blocks: int32 [8, 8, 34], replicated, may hold values from 0 to 63, as said below
- col_blocks: int32 [8, 8, 34], replicated, may hold values from 0 to 63, as said below
- live_counts: int32 [8, 8], replicated, may hold values from 30 to 34, as said below
- cotangent: bfloat16 [4096, 8192], P('seq', 'mp'), may hold values from -6 to 6
Outputs:
- outputs: bfloat16 [4096, 8192], P('seq', 'mp')
- context_grad: bfloat16 [16, 256, 8192], P(None, 'mp', 'seq')
- weight_grad: bfloat16 [8, 8, 34, 128, 128], P('mp', None, None, 'seq')
The draws below stay inside these ranges and needn't reach their ends.
Inputs may be any that keep to these rules, and one draw needn't show every extreme that they name: Owner o holds block columns o * 8 to o * 8 + 7 and owner j block rows j * 8 to j * 8 + 7; the slots of pair (o, j) name blocks in those ranges, with the block at row_blocks[o, j, k] and col_blocks[o, j, k], all slots of a pair naming distinct blocks. Only the first live_counts[o, j] slots are kept; the others are padding. `col_blocks`: see row_blocks. In every draw there is an owner j with live_counts[o, j] = 34 for every o.
All inputs are finite; a program needn't handle non-finite values.
Results may differ from the reference program's by a relative error of at most 0.001.
Values may be sent and summed in bfloat16 or wider, within the bound.
No kernel may reach another device: no remote copies, remote signals or barrier semaphores. Data moves between devices by JAX's collectives and lax.ppermute only.
A program may use at most 192 MiB of HBM per device.

```python
import math
import jax
import jax.numpy as jnp
from jax import lax

D = 8192
BLK = 128
TOK_DEV = 256
NB = 64
RB = 8
CAP = 34
CAP_MIN = 30
TOKENS = 4096
N_SEQ = 16
N_MP = 8


def kept_positions(key):
    region_keys = jax.random.split(key, N_MP * N_MP)
    orders = jax.vmap(lambda region_key: jax.random.permutation(region_key, jnp.arange(RB * RB, dtype=jnp.int32)))(region_keys)
    return orders[:, :CAP].reshape(N_MP, N_MP, CAP).astype(jnp.int32)


def draw_row_blocks(key, part):
    positions = kept_positions(key)
    owners = jnp.arange(N_MP, dtype=jnp.int32)[None, :, None]
    return (owners * RB + positions // RB).astype(jnp.int32)


def draw_col_blocks(key, part):
    positions = kept_positions(key)
    owners = jnp.arange(N_MP, dtype=jnp.int32)[:, None, None]
    return (owners * RB + positions % RB).astype(jnp.int32)


def draw_live_counts(key, part):
    key = jax.random.fold_in(key, 3)
    base_key, full_key = jax.random.split(key)
    base = jax.random.randint(base_key, (N_MP, N_MP), CAP_MIN, CAP + 1, dtype=jnp.int32)
    full_owner = jax.random.randint(full_key, (), 0, N_MP, dtype=jnp.int32)
    owners = jnp.arange(N_MP, dtype=jnp.int32)[None, :]
    return jnp.where(owners == full_owner, CAP, base).astype(jnp.int32)


def block_scale(rng, dims, pieces, smallest, high):
    loudness, own = 1.0, jax.random.fold_in(rng, 6)
    for position, shards_of in pieces:
        draws = jnp.exp(jax.random.uniform(jax.random.fold_in(own, position), (shards_of,), jnp.float32, smallest / len(pieces), high / len(pieces)))
        loudness = loudness * jnp.repeat(draws, dims[position] // shards_of).reshape([-1 if axis == position else 1 for axis in range(len(dims))])
    return loudness


def centred(stream_key, dims, width, reach, pieces=(), kind=jnp.bfloat16):
    array = jax.random.normal(stream_key, dims, jnp.float32) * width
    if len(pieces) > 0:
        array = block_scale(stream_key, dims, pieces, -0.22, 0.18) * array
    return jnp.clip(array, min=-reach, max=reach).astype(kind)


def setup_inputs(seed: int = 0) -> dict:
    arg_keys = jax.random.split(jax.random.key(seed), 7)
    context = centred(arg_keys[0], (N_SEQ, TOK_DEV, D), 1.0, 6.0, ((1, 8), (2, 16)))
    blocks = centred(arg_keys[1], (N_MP, N_MP, CAP, BLK, BLK), (D // 2) ** -0.5, 0.09375, ((0, 8),))
    row_blocks = draw_row_blocks(jax.random.fold_in(arg_keys[6], 71), 0)
    col_blocks = draw_col_blocks(jax.random.fold_in(arg_keys[6], 71), 0)
    live_counts = draw_live_counts(jax.random.fold_in(arg_keys[6], 71), 0)
    cotangent = centred(arg_keys[5], (TOKENS, D), 1.0, 6.0, ((0, 16), (1, 8)))
    return dict(context=context, blocks=blocks, row_blocks=row_blocks, col_blocks=col_blocks, live_counts=live_counts, cotangent=cotangent)


def dense_weight(blocks, row_blocks, col_blocks, live_counts):
    slot_ids = jnp.arange(CAP, dtype=jnp.int32)
    live = (slot_ids[None, None, :] < live_counts[:, :, None]).astype(jnp.float32)
    kept = blocks.astype(jnp.float32) * live[:, :, :, None, None]
    grid = jnp.zeros((NB, NB, BLK, BLK), jnp.float32)
    grid = grid.at[row_blocks.reshape(-1), col_blocks.reshape(-1)].add(kept.reshape(-1, BLK, BLK))
    return (grid.transpose(0, 2, 1, 3).reshape(D, D), live)

def reference(context, blocks, row_blocks, col_blocks, live_counts, cotangent):
    weight, live = dense_weight(blocks, row_blocks, col_blocks, live_counts)
    tokens = context.reshape(TOKENS, D).astype(jnp.float32)
    cot_values = cotangent.astype(jnp.float32)
    outputs = jnp.dot(tokens, weight, precision=lax.Precision.HIGHEST).astype(jnp.bfloat16)
    context_grad = jnp.dot(cot_values, weight.T, precision=lax.Precision.HIGHEST).astype(jnp.bfloat16)
    context_grad = context_grad.reshape(N_SEQ, TOK_DEV, D)
    grad_full = jnp.dot(tokens.T, cot_values, precision=lax.Precision.HIGHEST)
    grid = grad_full.reshape(NB, BLK, NB, BLK)
    picked = grid[row_blocks, :, col_blocks, :]
    weight_grad = (picked * live[:, :, :, None, None] * (1.0 / math.sqrt(TOKENS))).astype(jnp.bfloat16)
    return (outputs, context_grad, weight_grad)
```

```python
import functools
import math

import jax
import jax.numpy as jnp
from jax import lax
from jax.experimental import pallas as pl
from jax.experimental.pallas import tpu as pltpu
from jax.sharding import PartitionSpec as P

F32 = jnp.float32
BF16 = jnp.bfloat16
VMEM_LIMIT = 56 * 1024 * 1024


def build_panel(panel, blk_ref, rows_ref, cols_ref, live_ref, owner, j):
    panel[...] = jnp.zeros_like(panel)

    def place(k, carry):
        r = pl.multiple_of((rows_ref[owner, j, k] - 8 * j) * 128, 128)
        c = pl.multiple_of((cols_ref[owner, j, k] - 8 * owner) * 128, 128)
        panel[pl.ds(r, 128), pl.ds(c, 128)] = blk_ref[0, 0, k]
        return carry

    lax.fori_loop(0, live_ref[owner, j], place, 0)


def transpose_kernel(x_ref, o_ref):
    x = x_ref[...].reshape(512, 512).astype(F32)
    t = x.T.reshape(4, 16, 8, 512)
    for cls in range(16):
        o_ref[cls] = t[:, cls].reshape(32, 512).astype(BF16)


def partial_kernel(pos, rows, cols, live, cot_ref, blk_ref, keep, send0, send1, send2, send3, lhs, panel):
    j = pl.program_id(0)
    owner = pos[0]
    y = owner // 2
    core = owner % 2
    sends = (send0, send1, send2, send3)

    @pl.when(j == 0)
    def _():
        for d in range(4):
            group = (y + d) % 4
            lhs[pl.ds(d * 32, 32)] = cot_ref[group, core]
            lhs[pl.ds(128 + d * 32, 32)] = cot_ref[group, 1 - core]

    build_panel(panel, blk_ref, rows, cols, live, owner, j)
    for n in range(4):
        res = lax.dot_general(
            lhs[...], panel[pl.ds(n * 256, 256)], (((1,), (1,)), ((), ())), preferred_element_type=F32
        )
        half, lane = n // 2, (n % 2) * 256
        for d in range(4):
            keep[d, half, :, pl.ds(lane, 256)] = res[d * 32 : d * 32 + 32]
            sends[d][half, :, pl.ds(lane, 256)] = res[128 + d * 32 : 128 + d * 32 + 32]


def place_chunks(lhs, group, core, x, halves):
    start = pl.multiple_of((group * 2 + core) * 32, 32)
    for h in range(halves):
        lhs[pl.ds(start, 32), pl.ds(h * 512, 512)] = x[h]


def out_kernel(pos, rows, cols, live, a0, am, ap, a2a, a2b, b0, bm, bp, b2a, b2b, blk_ref, out_ref, lhs, panel, acc):
    j = pl.program_id(0)
    owner = pos[0]
    y = owner // 2
    core = owner % 2
    for who, (x0, xm, xp, x2a, x2b) in ((core, (a0, am, ap, a2a, a2b)), (1 - core, (b0, bm, bp, b2a, b2b))):
        place_chunks(lhs, y, who, x0, 2)
        place_chunks(lhs, (y + 3) % 4, who, xm, 2)
        place_chunks(lhs, (y + 1) % 4, who, xp, 2)

        @pl.when(j < 4)
        def _():
            place_chunks(lhs, (y + 2) % 4, who, x2a, 2)

        @pl.when(j >= 4)
        def _():
            place_chunks(lhs, (y + 2) % 4, who, x2b, 2)

    build_panel(panel, blk_ref, rows, cols, live, owner, j)
    for n in range(4):
        lanes = pl.ds(n * 256, 256)
        res = jnp.dot(lhs[...], panel[:, lanes], preferred_element_type=F32)

        @pl.when(j == 0)
        def _():
            acc[:, lanes] = res

        @pl.when((j > 0) & (j < 7))
        def _():
            acc[:, lanes] += res

        @pl.when(j == 7)
        def _():
            out_ref[:, lanes] = (acc[:, lanes] + res).astype(BF16)


def grad_kernel(scale, pos, rows, cols, live, a0, am, ap, a2a, a2b, b0, bm, bp, b2a, b2b, g_ref, out_ref, lhs, acc):
    i = pl.program_id(0)
    owner = pos[0]
    full = (a0, am, ap, None, b0, bm, bp, None)
    for at in range(8):

        @pl.when(i == at)
        def _():
            if full[at] is not None:
                lhs[...] = full[at][...].reshape(512, 512)
            else:
                first, second = (a2a, a2b) if at == 3 else (b2a, b2b)
                lhs[pl.ds(0, 256)] = first[...].reshape(256, 512)
                lhs[pl.ds(256, 256)] = second[...].reshape(256, 512)

    g = g_ref[...].reshape(512, 1024)
    for n in range(4):
        lanes = pl.ds(n * 256, 256)
        res = jnp.dot(lhs[...], g[:, n * 256 : n * 256 + 256], preferred_element_type=F32).reshape(64, 8, 256)

        @pl.when(i == 0)
        def _():
            acc[:, :, lanes] = res

        @pl.when(i > 0)
        def _():
            acc[:, :, lanes] += res

    @pl.when(i == 7)
    def _():
        def pick(j, carry):
            count = live[owner, j]

            def one(k, carry):
                r = rows[owner, j, k]
                c = pl.multiple_of((cols[owner, j, k] - 8 * owner) * 128, 128)
                tile = acc[r, :, pl.ds(c, 128)] * scale
                out_ref[0, j, k] = jnp.where(k < count, tile, 0.0).astype(BF16)
                return carry

            return lax.fori_loop(0, 34, one, carry, unroll=2)

        lax.fori_loop(0, 8, pick, 0)


def on_device(context, blocks, row_blocks, col_blocks, live_counts, cotangent):
    owner = lax.axis_index("mp")
    pos = owner.astype(jnp.int32).reshape(1)
    tables = (pos, row_blocks, col_blocks, live_counts)
    params = pltpu.CompilerParams(vmem_limit_bytes=VMEM_LIMIT)

    def along_y(x, step):
        return lax.ppermute(x, "mp", [(i, (i + 2 * step) % 8) for i in range(8)])

    def other_core(x):
        return lax.ppermute(x, "mp", [(i, i ^ 1) for i in range(8)])

    def exchange(x):
        return lax.all_to_all(x, "seq", split_axis=0, concat_axis=0, tiled=True)

    def gather_pieces(x):
        xm = along_y(x, 1)
        xp = along_y(x, -1)
        x2a = along_y(xm[:8], 1)
        x2b = along_y(xp[8:], -1)
        own = (x, xm, xp, x2a, x2b)
        return own + tuple(other_core(piece) for piece in own)

    blk_spec = pl.BlockSpec((1, 1, 34, 128, 128), lambda j, *_: (0, j, 0, 0, 0))
    part = jax.ShapeDtypeStruct((16, 32, 512), F32)
    part_spec = pl.BlockSpec((2, 32, 512), lambda j, *_: (j, 0, 0))
    keep, *sends = pl.pallas_call(
        partial_kernel,
        grid_spec=pltpu.PrefetchScalarGridSpec(
            num_scalar_prefetch=4,
            grid=(8,),
            in_specs=[pl.BlockSpec((4, 2, 32, 1024), lambda j, *_: (0, 0, 0, 0)), blk_spec],
            out_specs=[pl.BlockSpec((4, 2, 32, 512), lambda j, *_: (0, j, 0, 0))] + [part_spec] * 4,
            scratch_shapes=[pltpu.VMEM((256, 1024), BF16), pltpu.VMEM((1024, 1024), BF16)],
        ),
        out_shape=[jax.ShapeDtypeStruct((4, 16, 32, 512), F32)] + [part] * 4,
        compiler_params=params,
        cost_estimate=pl.CostEstimate(flops=4_300_000_000, bytes_accessed=18_000_000, transcendentals=0),
        name="partial_context_grad",
    )(*tables, cotangent.reshape(4, 2, 32, 1024), blocks)

    r2, r1, r3, r0 = (other_core(sends[d]) for d in (2, 1, 3, 0))
    from_a = along_y(keep[2, :8] + r2[:8], 1)
    from_b = along_y(keep[2, 8:] + r2[8:], -1)
    near_b = along_y(keep[1, 8:] + r1[8:], 1)
    near_a = along_y(keep[3, :8] + r3[:8], -1)
    far_a = along_y(keep[1, :8] + r1[:8] + from_a, 1)
    far_b = along_y(keep[3, 8:] + r3[8:] + from_b, -1)
    sum_a = keep[0, :8] + r0[:8] + near_a + far_a
    sum_b = keep[0, 8:] + r0[8:] + near_b + far_b
    context_grad = exchange(jnp.concatenate([sum_a, sum_b], axis=0).astype(BF16))

    x_pieces = gather_pieces(exchange(context))
    whole = pl.BlockSpec((2, 32, 512), lambda j, *_: (j, 0, 0))
    low = pl.BlockSpec((2, 32, 512), lambda j, *_: (jnp.minimum(j, 3), 0, 0))
    high = pl.BlockSpec((2, 32, 512), lambda j, *_: (jnp.maximum(j - 4, 0), 0, 0))
    outputs = pl.pallas_call(
        out_kernel,
        grid_spec=pltpu.PrefetchScalarGridSpec(
            num_scalar_prefetch=4,
            grid=(8,),
            in_specs=[whole, whole, whole, low, high] * 2 + [blk_spec],
            out_specs=pl.BlockSpec((256, 1024), lambda j, *_: (0, 0)),
            scratch_shapes=[
                pltpu.VMEM((256, 1024), BF16),
                pltpu.VMEM((1024, 1024), BF16),
                pltpu.VMEM((256, 1024), F32),
            ],
        ),
        out_shape=jax.ShapeDtypeStruct((256, 1024), BF16),
        compiler_params=params,
        cost_estimate=pl.CostEstimate(flops=4_300_000_000, bytes_accessed=14_000_000, transcendentals=0),
        name="outputs",
    )(*tables, *x_pieces, blocks)

    by_class = pl.pallas_call(
        transpose_kernel,
        out_shape=jax.ShapeDtypeStruct((16, 32, 512), BF16),
        compiler_params=params,
        name="feature_rows",
    )(context)
    t_pieces = gather_pieces(exchange(by_class))
    cot_all = lax.all_gather(cotangent, "seq", axis=0, tiled=True)
    full = pl.BlockSpec((16, 32, 512), lambda i, *_: (0, 0, 0))
    part8 = pl.BlockSpec((8, 32, 512), lambda i, *_: (0, 0, 0))

    def group_of(i, pos, *_):
        owner = pos[0]
        step = lax.rem(i, 4)
        shift = jnp.where(step == 1, 3, jnp.where(step == 2, 1, jnp.where(step == 3, 2, 0)))
        chip = lax.rem(lax.div(owner, 2) + shift, 4)
        core = lax.rem(owner + lax.div(i, 4), 2)
        return (0, chip * 2 + core, 0, 0)

    weight_grad = pl.pallas_call(
        functools.partial(grad_kernel, 1.0 / math.sqrt(4096)),
        grid_spec=pltpu.PrefetchScalarGridSpec(
            num_scalar_prefetch=4,
            grid=(8,),
            in_specs=[full, full, full, part8, part8] * 2 + [pl.BlockSpec((16, 1, 32, 1024), group_of)],
            out_specs=pl.BlockSpec((1, 8, 34, 8, 128), lambda i, *_: (0, 0, 0, 0, 0)),
            scratch_shapes=[pltpu.VMEM((512, 512), BF16), pltpu.VMEM((64, 8, 1024), F32)],
        ),
        out_shape=jax.ShapeDtypeStruct((1, 8, 34, 8, 128), BF16),
        compiler_params=params,
        cost_estimate=pl.CostEstimate(flops=4_300_000_000, bytes_accessed=14_000_000, transcendentals=0),
        name="weight_grad",
    )(*tables, *t_pieces, cot_all.reshape(16, 8, 32, 1024))
    return (outputs, context_grad, weight_grad)


def solution(mesh):
    in_specs = (
        P(None, "mp", "seq"),
        P("mp", None, None, None, None),
        P(),
        P(),
        P(),
        P("seq", "mp"),
    )
    out_specs = (P("seq", "mp"), P(None, "mp", "seq"), P("mp", None, None, "seq", None))
    return jax.shard_map(
        on_device, mesh=mesh, in_specs=in_specs, out_specs=out_specs, check_vma=False
    )
```

```python
import functools
import math

import jax
import jax.numpy as jnp
from jax import lax
from jax.experimental import pallas as pl
from jax.experimental.pallas import tpu as pltpu
from jax.sharding import PartitionSpec as P

F32 = jnp.float32
BF16 = jnp.bfloat16
VMEM_LIMIT = 60 * 1024 * 1024


def build_panel(panel, blk_ref, rows_ref, cols_ref, live_ref, owner, j):
    panel[...] = jnp.zeros_like(panel)
    count = live_ref[owner, j]
    for k in range(34):

        def place(k=k):
            r = pl.multiple_of((rows_ref[owner, j, k] - 8 * j) * 128, 128)
            c = pl.multiple_of((cols_ref[owner, j, k] - 8 * owner) * 128, 128)
            panel[pl.ds(r, 128), pl.ds(c, 128)] = blk_ref[0, 0, k]

        if k < 30:
            place()
        else:
            pl.when(k < count)(place)


def transpose_kernel(x_ref, o_ref):
    x = x_ref[...].reshape(512, 512).astype(F32)
    t = x.T.reshape(4, 16, 8, 512)
    for part in range(16):
        o_ref[part, pl.ds(0, 32)] = x_ref[part]
        o_ref[part, pl.ds(32, 32)] = t[:, part].reshape(32, 512).astype(BF16)


def partial_kernel(pos, rows, cols, live, cot_ref, blk_ref, keep, send0, send1, send2, send3, lhs, panel):
    j = pl.program_id(0)
    owner = pos[0]
    y = owner // 2
    core = owner % 2
    sends = (send0, send1, send2, send3)

    @pl.when(j == 0)
    def _():
        for d in range(4):
            group = (y + d) % 4
            lhs[pl.ds(d * 32, 32)] = cot_ref[group, core]
            lhs[pl.ds(128 + d * 32, 32)] = cot_ref[group, 1 - core]

    build_panel(panel, blk_ref, rows, cols, live, owner, j)
    res = lax.dot_general(lhs[...], panel[...], (((1,), (1,)), ((), ())), preferred_element_type=F32)
    for half in range(2):
        lanes = slice(half * 512, half * 512 + 512)
        for d in range(4):
            keep[d, half] = res[d * 32 : d * 32 + 32, lanes]
            sends[d][half] = res[128 + d * 32 : 128 + d * 32 + 32, lanes]


def place_chunks(lhs, group, core, x, halves):
    start = pl.multiple_of((group * 2 + core) * 32, 32)
    for h in range(halves):
        lhs[pl.ds(start, 32), pl.ds(h * 512, 512)] = x[h]


def out_kernel(pos, rows, cols, live, a0, am, ap, a2a, a2b, b0, bm, bp, b2a, b2b, blk_ref, out_ref, lhs, panel, acc):
    j = pl.program_id(0)
    owner = pos[0]
    y = owner // 2
    core = owner % 2
    for who, (x0, xm, xp, x2a, x2b) in ((core, (a0, am, ap, a2a, a2b)), (1 - core, (b0, bm, bp, b2a, b2b))):
        place_chunks(lhs, y, who, x0, 2)
        place_chunks(lhs, (y + 3) % 4, who, xm, 2)
        place_chunks(lhs, (y + 1) % 4, who, xp, 2)

        @pl.when(j < 4)
        def _():
            place_chunks(lhs, (y + 2) % 4, who, x2a, 2)

        @pl.when(j >= 4)
        def _():
            place_chunks(lhs, (y + 2) % 4, who, x2b, 2)

    @pl.when(j == 0)
    def _():
        acc[...] = jnp.zeros_like(acc)

    build_panel(panel, blk_ref, rows, cols, live, owner, j)
    acc[...] += jnp.dot(lhs[...], panel[...], preferred_element_type=F32)

    @pl.when(j == 7)
    def _():
        out_ref[...] = acc[...].astype(BF16)


def near_grad_kernel(pos, a0, am, ap, b0, bm, bp, g_ref, acc, lhs):
    i = pl.program_id(0)
    for at, piece in enumerate((a0, am, ap, b0, bm, bp)):

        @pl.when(i == at)
        def _(piece=piece):
            lhs[...] = piece[...].reshape(512, 512)

    @pl.when(i == 0)
    def _():
        acc[...] = jnp.zeros_like(acc)

    res = jnp.dot(lhs[...], g_ref[...].reshape(512, 1024), preferred_element_type=F32)
    acc[...] += res.reshape(64, 8, 1024)


def far_grad_kernel(scale, pos, rows, cols, live, a2a, a2b, b2a, b2b, g_ref, near_ref, out_ref, lhs, acc):
    i = pl.program_id(0)
    owner = pos[0]
    for at, (first, second) in enumerate(((a2a, a2b), (b2a, b2b))):

        @pl.when(i == at)
        def _(first=first, second=second):
            lhs[pl.ds(0, 256)] = first[...].reshape(256, 512)
            lhs[pl.ds(256, 256)] = second[...].reshape(256, 512)

    @pl.when(i == 0)
    def _():
        acc[...] = near_ref[...]

    res = jnp.dot(lhs[...], g_ref[...].reshape(512, 1024), preferred_element_type=F32)
    acc[...] += res.reshape(64, 8, 1024)

    @pl.when(i == 1)
    def _():
        def pick(j, carry):
            count = live[owner, j]
            for k in range(34):
                r = rows[owner, j, k]
                c = pl.multiple_of((cols[owner, j, k] - 8 * owner) * 128, 128)
                tile = acc[r, :, pl.ds(c, 128)] * scale
                if k >= 30:
                    tile = jnp.where(k < count, tile, 0.0)
                out_ref[0, j, k] = tile.astype(BF16)
            return carry

        lax.fori_loop(0, 8, pick, 0)


def on_device(context, blocks, row_blocks, col_blocks, live_counts, cotangent):
    owner = lax.axis_index("mp")
    pos = owner.astype(jnp.int32).reshape(1)
    tables = (pos, row_blocks, col_blocks, live_counts)
    params = pltpu.CompilerParams(vmem_limit_bytes=VMEM_LIMIT)
    barrier = lax.optimization_barrier

    def cost(flops, size):
        return pl.CostEstimate(flops=flops, bytes_accessed=size, transcendentals=0)

    def along_y(x, step):
        return lax.ppermute(x, "mp", [(i, (i + 2 * step) % 8) for i in range(8)])

    def other_core(x):
        return lax.ppermute(x, "mp", [(i, i ^ 1) for i in range(8)])

    def exchange(x):
        return lax.all_to_all(x, "seq", split_axis=0, concat_axis=0, tiled=True)

    cot_all = lax.all_gather(cotangent, "seq", axis=0, tiled=True)

    both = pl.pallas_call(
        transpose_kernel,
        out_shape=jax.ShapeDtypeStruct((16, 64, 512), BF16),
        compiler_params=params,
        name="feature_rows",
    )(context)
    both = exchange(both)
    tokens, class_rows = both[:, :32], both[:, 32:]

    blk_spec = pl.BlockSpec((1, 1, 34, 128, 128), lambda j, *_: (0, j, 0, 0, 0))
    part = jax.ShapeDtypeStruct((16, 32, 512), F32)
    part_spec = pl.BlockSpec((2, 32, 512), lambda j, *_: (j, 0, 0))
    keep, *sends = pl.pallas_call(
        partial_kernel,
        grid_spec=pltpu.PrefetchScalarGridSpec(
            num_scalar_prefetch=4,
            grid=(8,),
            in_specs=[pl.BlockSpec((4, 2, 32, 1024), lambda j, *_: (0, 0, 0, 0)), blk_spec],
            out_specs=[pl.BlockSpec((4, 2, 32, 512), lambda j, *_: (0, j, 0, 0))] + [part_spec] * 4,
            scratch_shapes=[pltpu.VMEM((256, 1024), BF16), pltpu.VMEM((1024, 1024), BF16)],
        ),
        out_shape=[jax.ShapeDtypeStruct((4, 16, 32, 512), F32)] + [part] * 4,
        compiler_params=params,
        cost_estimate=cost(4_300_000_000, 18_000_000),
        name="partial_context_grad",
    )(*tables, cotangent.reshape(4, 2, 32, 1024), blocks)
    r2, r1, r3, r0 = (other_core(sends[d]) for d in (2, 1, 3, 0))

    xm, xp = along_y(tokens, 1), along_y(tokens, -1)

    q2a, q2b = keep[2, :8] + r2[:8], keep[2, 8:] + r2[8:]
    q1b, q3a = keep[1, 8:] + r1[8:], keep[3, :8] + r3[:8]
    q2a, q2b, q1b, q3a, class_rows = barrier((q2a, q2b, q1b, q3a, class_rows))
    from_a, from_b = along_y(q2a, 1), along_y(q2b, -1)
    near_b, near_a = along_y(q1b, 1), along_y(q3a, -1)

    x2a, x2b = along_y(xm[:8], 1), along_y(xp[8:], -1)
    own = (tokens, xm, xp, x2a, x2b)
    x_pieces = own + tuple(other_core(piece) for piece in own)

    cm, cp = along_y(class_rows, 1), along_y(class_rows, -1)

    q1a, q3b = keep[1, :8] + r1[:8] + from_a, keep[3, 8:] + r3[8:] + from_b
    q1a, q3b, x_pieces = barrier((q1a, q3b, x_pieces))
    far_a, far_b = along_y(q1a, 1), along_y(q3b, -1)

    whole = pl.BlockSpec((2, 32, 512), lambda j, *_: (j, 0, 0))
    low = pl.BlockSpec((2, 32, 512), lambda j, *_: (jnp.minimum(j, 3), 0, 0))
    high = pl.BlockSpec((2, 32, 512), lambda j, *_: (jnp.maximum(j - 4, 0), 0, 0))
    outputs = pl.pallas_call(
        out_kernel,
        grid_spec=pltpu.PrefetchScalarGridSpec(
            num_scalar_prefetch=4,
            grid=(8,),
            in_specs=[whole, whole, whole, low, high] * 2 + [blk_spec],
            out_specs=pl.BlockSpec((256, 1024), lambda j, *_: (0, 0)),
            scratch_shapes=[
                pltpu.VMEM((256, 1024), BF16),
                pltpu.VMEM((1024, 1024), BF16),
                pltpu.VMEM((256, 1024), F32),
            ],
        ),
        out_shape=jax.ShapeDtypeStruct((256, 1024), BF16),
        compiler_params=params,
        cost_estimate=cost(4_300_000_000, 14_000_000),
        name="outputs",
    )(*tables, *x_pieces, blocks)

    outputs, cm, cp = barrier((outputs, cm, cp))
    c2a, c2b = along_y(cm[:8], 1), along_y(cp[8:], -1)

    near = (class_rows, cm, cp)
    near = near + tuple(other_core(piece) for piece in near)
    full = pl.BlockSpec((16, 32, 512), lambda i, *_: (0, 0, 0))
    part8 = pl.BlockSpec((8, 32, 512), lambda i, *_: (0, 0, 0))
    cot_groups = cot_all.reshape(16, 8, 32, 1024)

    def group(owner, chip_step, core_step):
        return lax.rem(lax.div(owner, 2) + chip_step, 4) * 2 + lax.rem(owner + core_step, 2)

    def near_group(i, pos):
        step = lax.rem(i, 3)
        chip_step = jnp.where(step == 1, 3, jnp.where(step == 2, 1, 0))
        return (0, group(pos[0], chip_step, lax.div(i, 3)), 0, 0)

    def far_group(i, pos, *_):
        return (0, group(pos[0], 2, i), 0, 0)

    total = jax.ShapeDtypeStruct((64, 8, 1024), F32)
    total_spec = pl.BlockSpec((64, 8, 1024), lambda i, *_: (0, 0, 0))
    near_grad = pl.pallas_call(
        near_grad_kernel,
        grid_spec=pltpu.PrefetchScalarGridSpec(
            num_scalar_prefetch=1,
            grid=(6,),
            in_specs=[full] * 6 + [pl.BlockSpec((16, 1, 32, 1024), near_group)],
            out_specs=total_spec,
            scratch_shapes=[pltpu.VMEM((512, 512), BF16)],
        ),
        out_shape=total,
        compiler_params=params,
        cost_estimate=cost(3_200_000_000, 11_000_000),
        name="near_weight_grad",
    )(pos, *near, cot_groups)

    sum_a = keep[0, :8] + r0[:8] + near_a + far_a
    sum_b = keep[0, 8:] + r0[8:] + near_b + far_b
    context_sum = jnp.concatenate([sum_a, sum_b], axis=0).astype(BF16)
    context_sum, near_grad = barrier((context_sum, near_grad))
    context_grad = exchange(context_sum)

    weight_grad = pl.pallas_call(
        functools.partial(far_grad_kernel, 1.0 / math.sqrt(4096)),
        grid_spec=pltpu.PrefetchScalarGridSpec(
            num_scalar_prefetch=4,
            grid=(2,),
            in_specs=[part8] * 4 + [pl.BlockSpec((16, 1, 32, 1024), far_group), total_spec],
            out_specs=pl.BlockSpec((1, 8, 34, 8, 128), lambda i, *_: (0, 0, 0, 0, 0)),
            scratch_shapes=[pltpu.VMEM((512, 512), BF16), pltpu.VMEM((64, 8, 1024), F32)],
        ),
        out_shape=jax.ShapeDtypeStruct((1, 8, 34, 8, 128), BF16),
        compiler_params=params,
        cost_estimate=cost(1_100_000_000, 6_000_000),
        name="far_weight_grad",
    )(*tables, c2a, c2b, other_core(c2a), other_core(c2b), cot_groups, near_grad)
    return (outputs, context_grad, weight_grad)


def solution(mesh):
    in_specs = (
        P(None, "mp", "seq"),
        P("mp", None, None, None, None),
        P(),
        P(),
        P(),
        P("seq", "mp"),
    )
    out_specs = (P("seq", "mp"), P(None, "mp", "seq"), P("mp", None, None, "seq", None))
    return jax.shard_map(
        on_device, mesh=mesh, in_specs=in_specs, out_specs=out_specs, check_vma=False
    )
```

```python
import functools
import math

import jax
import jax.numpy as jnp
from jax import lax
from jax.experimental import pallas as pl
from jax.experimental.pallas import tpu as pltpu
from jax.sharding import PartitionSpec as P

F32 = jnp.float32
BF16 = jnp.bfloat16
VMEM_LIMIT = 60 * 1024 * 1024


def build_panel(panel, blk_ref, rows_ref, cols_ref, live_ref, owner, j):
    panel[...] = jnp.zeros_like(panel)
    count = live_ref[owner, j]
    for k in range(34):

        def place(k=k):
            r = pl.multiple_of((rows_ref[owner, j, k] - 8 * j) * 128, 128)
            c = pl.multiple_of((cols_ref[owner, j, k] - 8 * owner) * 128, 128)
            panel[pl.ds(r, 128), pl.ds(c, 128)] = blk_ref[0, 0, k]

        if k < 30:
            place()
        else:
            pl.when(k < count)(place)


def transpose_kernel(x_ref, o_ref):
    x = x_ref[...].reshape(512, 512).astype(F32)
    t = x.T.reshape(4, 16, 8, 512)
    for part in range(16):
        o_ref[part, pl.ds(0, 32)] = x_ref[part]
        o_ref[part, pl.ds(32, 32)] = t[:, part].reshape(32, 512).astype(BF16)


def partial_kernel(pos, rows, cols, live, cot_ref, blk_ref, keep, send0, send1, send2, send3, lhs, panel):
    j = pl.program_id(0)
    owner = pos[0]
    y = owner // 2
    core = owner % 2
    sends = (send0, send1, send2, send3)

    @pl.when(j == 0)
    def _():
        for d in range(4):
            group = (y + d) % 4
            lhs[pl.ds(d * 32, 32)] = cot_ref[group, core]
            lhs[pl.ds(128 + d * 32, 32)] = cot_ref[group, 1 - core]

    build_panel(panel, blk_ref, rows, cols, live, owner, j)
    res = lax.dot_general(lhs[...], panel[...], (((1,), (1,)), ((), ())), preferred_element_type=F32)
    for half in range(2):
        lanes = slice(half * 512, half * 512 + 512)
        for d in range(4):
            keep[d, half] = res[d * 32 : d * 32 + 32, lanes]
            sends[d][half] = res[128 + d * 32 : 128 + d * 32 + 32, lanes]


def place_chunks(lhs, group, core, x, halves):
    start = pl.multiple_of((group * 2 + core) * 32, 32)
    for h in range(halves):
        lhs[pl.ds(start, 32), pl.ds(h * 512, 512)] = x[h]


def out_kernel(pos, rows, cols, live, a0, am, ap, a2a, a2b, b0, bm, bp, b2a, b2b, blk_ref, out_ref, lhs, panel, acc):
    j = pl.program_id(0)
    owner = pos[0]
    y = owner // 2
    core = owner % 2
    for who, (x0, xm, xp, x2a, x2b) in ((core, (a0, am, ap, a2a, a2b)), (1 - core, (b0, bm, bp, b2a, b2b))):
        place_chunks(lhs, y, who, x0, 2)
        place_chunks(lhs, (y + 3) % 4, who, xm, 2)
        place_chunks(lhs, (y + 1) % 4, who, xp, 2)

        @pl.when(j < 4)
        def _():
            place_chunks(lhs, (y + 2) % 4, who, x2a, 2)

        @pl.when(j >= 4)
        def _():
            place_chunks(lhs, (y + 2) % 4, who, x2b, 2)

    @pl.when(j == 0)
    def _():
        acc[...] = jnp.zeros_like(acc)

    build_panel(panel, blk_ref, rows, cols, live, owner, j)
    acc[...] += jnp.dot(lhs[...], panel[...], preferred_element_type=F32)

    @pl.when(j == 7)
    def _():
        out_ref[...] = acc[...].astype(BF16)


def near_grad_kernel(pos, a0, am, ap, b0, bm, bp, g_ref, acc, lhs):
    i = pl.program_id(0)
    for at, piece in enumerate((a0, am, ap, b0, bm, bp)):

        @pl.when(i == at)
        def _(piece=piece):
            lhs[...] = piece[...].reshape(512, 512)

    @pl.when(i == 0)
    def _():
        acc[...] = jnp.zeros_like(acc)

    res = jnp.dot(lhs[...], g_ref[...].reshape(512, 1024), preferred_element_type=F32)
    acc[...] += res.reshape(64, 8, 1024)


def far_grad_kernel(scale, pos, rows, cols, live, a2a, a2b, b2a, b2b, g_ref, near_ref, out_ref, lhs, acc):
    i = pl.program_id(0)
    owner = pos[0]
    for at, (first, second) in enumerate(((a2a, a2b), (b2a, b2b))):

        @pl.when(i == at)
        def _(first=first, second=second):
            lhs[pl.ds(0, 256)] = first[...].reshape(256, 512)
            lhs[pl.ds(256, 256)] = second[...].reshape(256, 512)

    @pl.when(i == 0)
    def _():
        acc[...] = near_ref[...]

    res = jnp.dot(lhs[...], g_ref[...].reshape(512, 1024), preferred_element_type=F32)
    acc[...] += res.reshape(64, 8, 1024)

    @pl.when(i == 1)
    def _():
        def pick(j, carry):
            count = live[owner, j]
            for k in range(34):
                r = rows[owner, j, k]
                c = pl.multiple_of((cols[owner, j, k] - 8 * owner) * 128, 128)
                tile = acc[r, :, pl.ds(c, 128)] * scale
                if k >= 30:
                    tile = jnp.where(k < count, tile, 0.0)
                out_ref[0, j, k] = tile.astype(BF16)
            return carry

        lax.fori_loop(0, 8, pick, 0)


def on_device(context, blocks, row_blocks, col_blocks, live_counts, cotangent):
    owner = lax.axis_index("mp")
    pos = owner.astype(jnp.int32).reshape(1)
    tables = (pos, row_blocks, col_blocks, live_counts)
    params = pltpu.CompilerParams(vmem_limit_bytes=VMEM_LIMIT)
    barrier = lax.optimization_barrier

    def cost(flops, size):
        return pl.CostEstimate(flops=flops, bytes_accessed=size, transcendentals=0)

    def along_y(x, step):
        return lax.ppermute(x, "mp", [(i, (i + 2 * step) % 8) for i in range(8)])

    def other_core(x):
        return lax.ppermute(x, "mp", [(i, i ^ 1) for i in range(8)])

    def exchange(x):
        return lax.all_to_all(x, "seq", split_axis=0, concat_axis=0, tiled=True)

    cot_all = lax.all_gather(cotangent, "seq", axis=0, tiled=True)

    both = pl.pallas_call(
        transpose_kernel,
        out_shape=jax.ShapeDtypeStruct((16, 64, 512), BF16),
        compiler_params=params,
        name="feature_rows",
    )(context)
    both = exchange(both)
    tokens, class_rows = both[:, :32], both[:, 32:]

    blk_spec = pl.BlockSpec((1, 1, 34, 128, 128), lambda j, *_: (0, j, 0, 0, 0))
    part = jax.ShapeDtypeStruct((16, 32, 512), F32)
    part_spec = pl.BlockSpec((2, 32, 512), lambda j, *_: (j, 0, 0))
    keep, *sends = pl.pallas_call(
        partial_kernel,
        grid_spec=pltpu.PrefetchScalarGridSpec(
            num_scalar_prefetch=4,
            grid=(8,),
            in_specs=[pl.BlockSpec((4, 2, 32, 1024), lambda j, *_: (0, 0, 0, 0)), blk_spec],
            out_specs=[pl.BlockSpec((4, 2, 32, 512), lambda j, *_: (0, j, 0, 0))] + [part_spec] * 4,
            scratch_shapes=[pltpu.VMEM((256, 1024), BF16), pltpu.VMEM((1024, 1024), BF16)],
        ),
        out_shape=[jax.ShapeDtypeStruct((4, 16, 32, 512), F32)] + [part] * 4,
        compiler_params=params,
        cost_estimate=cost(4_300_000_000, 18_000_000),
        name="partial_context_grad",
    )(*tables, cotangent.reshape(4, 2, 32, 1024), blocks)
    r2, r1, r3, r0 = (other_core(sends[d]) for d in (2, 1, 3, 0))

    xm, xp = along_y(tokens, 1), along_y(tokens, -1)

    q2a, q2b, xm, xp = barrier((keep[2, :8] + r2[:8], keep[2, 8:] + r2[8:], xm, xp))
    x2a, x2b = along_y(xm[:8], 1), along_y(xp[8:], -1)
    from_a, from_b = along_y(q2a, 1), along_y(q2b, -1)
    own = (tokens, xm, xp, x2a, x2b)
    x_pieces = own + tuple(other_core(piece) for piece in own)

    q1b, q3a = keep[1, 8:] + r1[8:], keep[3, :8] + r3[:8]
    q1b, q3a, class_rows, x_pieces = barrier((q1b, q3a, class_rows, x_pieces))
    cm, cp = along_y(class_rows, 1), along_y(class_rows, -1)
    near_b, near_a = along_y(q1b, 1), along_y(q3a, -1)

    whole = pl.BlockSpec((2, 32, 512), lambda j, *_: (j, 0, 0))
    low = pl.BlockSpec((2, 32, 512), lambda j, *_: (jnp.minimum(j, 3), 0, 0))
    high = pl.BlockSpec((2, 32, 512), lambda j, *_: (jnp.maximum(j - 4, 0), 0, 0))
    outputs = pl.pallas_call(
        out_kernel,
        grid_spec=pltpu.PrefetchScalarGridSpec(
            num_scalar_prefetch=4,
            grid=(8,),
            in_specs=[whole, whole, whole, low, high] * 2 + [blk_spec],
            out_specs=pl.BlockSpec((256, 1024), lambda j, *_: (0, 0)),
            scratch_shapes=[
                pltpu.VMEM((256, 1024), BF16),
                pltpu.VMEM((1024, 1024), BF16),
                pltpu.VMEM((256, 1024), F32),
            ],
        ),
        out_shape=jax.ShapeDtypeStruct((256, 1024), BF16),
        compiler_params=params,
        cost_estimate=cost(4_300_000_000, 14_000_000),
        name="outputs",
    )(*tables, *x_pieces, blocks)

    outputs, cm, cp, from_a, from_b = barrier((outputs, cm, cp, from_a, from_b))
    q1a, q3b = keep[1, :8] + r1[:8] + from_a, keep[3, 8:] + r3[8:] + from_b
    far_a, far_b = along_y(q1a, 1), along_y(q3b, -1)

    c2a, c2b = along_y(cm[:8], 1), along_y(cp[8:], -1)

    near = (class_rows, cm, cp)
    near = near + tuple(other_core(piece) for piece in near)
    full = pl.BlockSpec((16, 32, 512), lambda i, *_: (0, 0, 0))
    part8 = pl.BlockSpec((8, 32, 512), lambda i, *_: (0, 0, 0))
    cot_groups = cot_all.reshape(16, 8, 32, 1024)

    def group(owner, chip_step, core_step):
        return lax.rem(lax.div(owner, 2) + chip_step, 4) * 2 + lax.rem(owner + core_step, 2)

    def near_group(i, pos):
        step = lax.rem(i, 3)
        chip_step = jnp.where(step == 1, 3, jnp.where(step == 2, 1, 0))
        return (0, group(pos[0], chip_step, lax.div(i, 3)), 0, 0)

    def far_group(i, pos, *_):
        return (0, group(pos[0], 2, i), 0, 0)

    total = jax.ShapeDtypeStruct((64, 8, 1024), F32)
    total_spec = pl.BlockSpec((64, 8, 1024), lambda i, *_: (0, 0, 0))
    near_grad = pl.pallas_call(
        near_grad_kernel,
        grid_spec=pltpu.PrefetchScalarGridSpec(
            num_scalar_prefetch=1,
            grid=(6,),
            in_specs=[full] * 6 + [pl.BlockSpec((16, 1, 32, 1024), near_group)],
            out_specs=total_spec,
            scratch_shapes=[pltpu.VMEM((512, 512), BF16)],
        ),
        out_shape=total,
        compiler_params=params,
        cost_estimate=cost(3_200_000_000, 11_000_000),
        name="near_weight_grad",
    )(pos, *near, cot_groups)

    sum_a = keep[0, :8] + r0[:8] + near_a + far_a
    sum_b = keep[0, 8:] + r0[8:] + near_b + far_b
    context_sum = jnp.concatenate([sum_a, sum_b], axis=0).astype(BF16)
    context_sum, near_grad = barrier((context_sum, near_grad))
    context_grad = exchange(context_sum)

    weight_grad = pl.pallas_call(
        functools.partial(far_grad_kernel, 1.0 / math.sqrt(4096)),
        grid_spec=pltpu.PrefetchScalarGridSpec(
            num_scalar_prefetch=4,
            grid=(2,),
            in_specs=[part8] * 4 + [pl.BlockSpec((16, 1, 32, 1024), far_group), total_spec],
            out_specs=pl.BlockSpec((1, 8, 34, 8, 128), lambda i, *_: (0, 0, 0, 0, 0)),
            scratch_shapes=[pltpu.VMEM((512, 512), BF16), pltpu.VMEM((64, 8, 1024), F32)],
        ),
        out_shape=jax.ShapeDtypeStruct((1, 8, 34, 8, 128), BF16),
        compiler_params=params,
        cost_estimate=cost(1_100_000_000, 6_000_000),
        name="far_weight_grad",
    )(*tables, c2a, c2b, other_core(c2a), other_core(c2b), cot_groups, near_grad)
    return (outputs, context_grad, weight_grad)


def solution(mesh):
    in_specs = (
        P(None, "mp", "seq"),
        P("mp", None, None, None, None),
        P(),
        P(),
        P(),
        P("seq", "mp"),
    )
    out_specs = (P("seq", "mp"), P(None, "mp", "seq"), P("mp", None, None, "seq", None))
    return jax.shard_map(
        on_device, mesh=mesh, in_specs=in_specs, out_specs=out_specs, check_vma=False
    )
```

```python
import functools
import math

import jax
import jax.numpy as jnp
from jax import lax
from jax.experimental import pallas as pl
from jax.experimental.pallas import tpu as pltpu
from jax.sharding import PartitionSpec as P

F32 = jnp.float32
BF16 = jnp.bfloat16
VMEM_LIMIT = 60 * 1024 * 1024


def build_panel(panel, blk_ref, rows_ref, cols_ref, live_ref, owner, j):
    panel[...] = jnp.zeros_like(panel)
    count = live_ref[owner, j]
    for k in range(34):

        def place(k=k):
            r = pl.multiple_of((rows_ref[owner, j, k] - 8 * j) * 128, 128)
            c = pl.multiple_of((cols_ref[owner, j, k] - 8 * owner) * 128, 128)
            panel[pl.ds(r, 128), pl.ds(c, 128)] = blk_ref[0, 0, k]

        if k < 30:
            place()
        else:
            pl.when(k < count)(place)


def transpose_kernel(x_ref, o_ref):
    x = x_ref[...].reshape(512, 512).astype(F32)
    t = x.T.reshape(4, 16, 8, 512)
    for part in range(16):
        o_ref[part, pl.ds(0, 32)] = x_ref[part]
        o_ref[part, pl.ds(32, 32)] = t[:, part].reshape(32, 512).astype(BF16)


def partial_kernel(pos, rows, cols, live, cot_ref, blk_ref, keep, across, rest, lhs, panel):
    j = pl.program_id(0)
    owner = pos[0]
    y = owner // 2
    core = owner % 2
    sends = (rest.at[0], rest.at[1], across, rest.at[2])

    @pl.when(j == 0)
    def _():
        for d in range(4):
            group = (y + d) % 4
            lhs[pl.ds(d * 32, 32)] = cot_ref[group, core]
            lhs[pl.ds(128 + d * 32, 32)] = cot_ref[group, 1 - core]

    build_panel(panel, blk_ref, rows, cols, live, owner, j)
    res = lax.dot_general(lhs[...], panel[...], (((1,), (1,)), ((), ())), preferred_element_type=F32)
    for half in range(2):
        lanes = slice(half * 512, half * 512 + 512)
        for d in range(4):
            keep[d, half] = res[d * 32 : d * 32 + 32, lanes]
            sends[d][half] = res[128 + d * 32 : 128 + d * 32 + 32, lanes]


def place_chunks(lhs, group, core, x, halves):
    start = pl.multiple_of((group * 2 + core) * 32, 32)
    for h in range(halves):
        lhs[pl.ds(start, 32), pl.ds(h * 512, 512)] = x[h]


def out_kernel(pos, rows, cols, live, a0, am, ap, a2a, a2b, b0, bm, bp, b2a, b2b, blk_ref, out_ref, lhs, panel, acc):
    j = pl.program_id(0)
    owner = pos[0]
    y = owner // 2
    core = owner % 2
    for who, (x0, xm, xp, x2a, x2b) in ((core, (a0, am, ap, a2a, a2b)), (1 - core, (b0, bm, bp, b2a, b2b))):
        place_chunks(lhs, y, who, x0, 2)
        place_chunks(lhs, (y + 3) % 4, who, xm, 2)
        place_chunks(lhs, (y + 1) % 4, who, xp, 2)

        @pl.when(j < 4)
        def _():
            place_chunks(lhs, (y + 2) % 4, who, x2a, 2)

        @pl.when(j >= 4)
        def _():
            place_chunks(lhs, (y + 2) % 4, who, x2b, 2)

    @pl.when(j == 0)
    def _():
        acc[...] = jnp.zeros_like(acc)

    build_panel(panel, blk_ref, rows, cols, live, owner, j)
    acc[...] += jnp.dot(lhs[...], panel[...], preferred_element_type=F32)

    @pl.when(j == 7)
    def _():
        out_ref[...] = acc[...].astype(BF16)


def near_grad_kernel(pos, a0, am, ap, b0, bm, bp, g_ref, acc, lhs):
    i = pl.program_id(0)
    for at, piece in enumerate((a0, am, ap, b0, bm, bp)):

        @pl.when(i == at)
        def _(piece=piece):
            lhs[...] = piece[...].reshape(512, 512)

    @pl.when(i == 0)
    def _():
        acc[...] = jnp.zeros_like(acc)

    res = jnp.dot(lhs[...], g_ref[...].reshape(512, 1024), preferred_element_type=F32)
    acc[...] += res.reshape(64, 8, 1024)


def far_grad_kernel(scale, pos, rows, cols, live, a2a, a2b, b2a, b2b, g_ref, near_ref, out_ref, lhs, acc):
    i = pl.program_id(0)
    owner = pos[0]
    for at, (first, second) in enumerate(((a2a, a2b), (b2a, b2b))):

        @pl.when(i == at)
        def _(first=first, second=second):
            lhs[pl.ds(0, 256)] = first[...].reshape(256, 512)
            lhs[pl.ds(256, 256)] = second[...].reshape(256, 512)

    @pl.when(i == 0)
    def _():
        acc[...] = near_ref[...]

    res = jnp.dot(lhs[...], g_ref[...].reshape(512, 1024), preferred_element_type=F32)
    acc[...] += res.reshape(64, 8, 1024)

    @pl.when(i == 1)
    def _():
        def pick(j, carry):
            count = live[owner, j]
            for k in range(34):
                r = rows[owner, j, k]
                c = pl.multiple_of((cols[owner, j, k] - 8 * owner) * 128, 128)
                tile = acc[r, :, pl.ds(c, 128)] * scale
                if k >= 30:
                    tile = jnp.where(k < count, tile, 0.0)
                out_ref[0, j, k] = tile.astype(BF16)
            return carry

        lax.fori_loop(0, 8, pick, 0)


def on_device(context, blocks, row_blocks, col_blocks, live_counts, cotangent):
    owner = lax.axis_index("mp")
    pos = owner.astype(jnp.int32).reshape(1)
    tables = (pos, row_blocks, col_blocks, live_counts)
    params = pltpu.CompilerParams(vmem_limit_bytes=VMEM_LIMIT)
    barrier = lax.optimization_barrier

    def cost(flops, size):
        return pl.CostEstimate(flops=flops, bytes_accessed=size, transcendentals=0)

    def along_y(x, step):
        return lax.ppermute(x, "mp", [(i, (i + 2 * step) % 8) for i in range(8)])

    def other_core(x):
        return lax.ppermute(x, "mp", [(i, i ^ 1) for i in range(8)])

    def exchange(x):
        return lax.all_to_all(x, "seq", split_axis=0, concat_axis=0, tiled=True)

    cot_all = lax.all_gather(cotangent, "seq", axis=0, tiled=True)

    both = pl.pallas_call(
        transpose_kernel,
        out_shape=jax.ShapeDtypeStruct((16, 64, 512), BF16),
        compiler_params=params,
        name="feature_rows",
    )(context)
    both, cot_own = barrier((both, cotangent))
    both = exchange(both)
    tokens, class_rows = both[:, :32], both[:, 32:]

    blk_spec = pl.BlockSpec((1, 1, 34, 128, 128), lambda j, *_: (0, j, 0, 0, 0))
    keep, across, rest = pl.pallas_call(
        partial_kernel,
        grid_spec=pltpu.PrefetchScalarGridSpec(
            num_scalar_prefetch=4,
            grid=(8,),
            in_specs=[pl.BlockSpec((4, 2, 32, 1024), lambda j, *_: (0, 0, 0, 0)), blk_spec],
            out_specs=[
                pl.BlockSpec((4, 2, 32, 512), lambda j, *_: (0, j, 0, 0)),
                pl.BlockSpec((2, 32, 512), lambda j, *_: (j, 0, 0)),
                pl.BlockSpec((3, 2, 32, 512), lambda j, *_: (0, j, 0, 0)),
            ],
            scratch_shapes=[pltpu.VMEM((256, 1024), BF16), pltpu.VMEM((1024, 1024), BF16)],
        ),
        out_shape=[
            jax.ShapeDtypeStruct((4, 16, 32, 512), F32),
            jax.ShapeDtypeStruct((16, 32, 512), F32),
            jax.ShapeDtypeStruct((3, 16, 32, 512), F32),
        ],
        compiler_params=params,
        cost_estimate=cost(4_300_000_000, 52_000_000),
        name="partial_context_grad",
    )(*tables, cot_own.reshape(4, 2, 32, 1024), blocks)
    across = other_core(across)

    xm, xp = along_y(tokens, 1), along_y(tokens, -1)
    rest, _ = barrier((rest, tokens))
    rest = other_core(rest)

    q2a, q2b, xm, xp = barrier((keep[2, :8] + across[:8], keep[2, 8:] + across[8:], xm, xp))
    xma, xpb, q2a, q2b = barrier((xm[:8], xp[8:], q2a, q2b))
    x2a, x2b = along_y(xma, 1), along_y(xpb, -1)
    from_a, from_b = along_y(q2a, 1), along_y(q2b, -1)
    own = (tokens, xm, xp, x2a, x2b)
    x_pieces = own + tuple(other_core(piece) for piece in own)

    class_rows, x2a, x2b = barrier((class_rows, x2a, x2b))
    cm, cp = along_y(class_rows, 1), along_y(class_rows, -1)

    q1 = jnp.concatenate([keep[1, :8] + rest[1, :8] + from_a, keep[1, 8:] + rest[1, 8:]], axis=0)
    q3 = jnp.concatenate([keep[3, :8] + rest[2, :8], keep[3, 8:] + rest[2, 8:] + from_b], axis=0)
    q1, q3, x_pieces = barrier((q1, q3, x_pieces))
    sum_m, sum_p = along_y(q1, 1), along_y(q3, -1)

    whole = pl.BlockSpec((2, 32, 512), lambda j, *_: (j, 0, 0))
    low = pl.BlockSpec((2, 32, 512), lambda j, *_: (jnp.minimum(j, 3), 0, 0))
    high = pl.BlockSpec((2, 32, 512), lambda j, *_: (jnp.maximum(j - 4, 0), 0, 0))
    outputs = pl.pallas_call(
        out_kernel,
        grid_spec=pltpu.PrefetchScalarGridSpec(
            num_scalar_prefetch=4,
            grid=(8,),
            in_specs=[whole, whole, whole, low, high] * 2 + [blk_spec],
            out_specs=pl.BlockSpec((256, 1024), lambda j, *_: (0, 0)),
            scratch_shapes=[
                pltpu.VMEM((256, 1024), BF16),
                pltpu.VMEM((1024, 1024), BF16),
                pltpu.VMEM((256, 1024), F32),
            ],
        ),
        out_shape=jax.ShapeDtypeStruct((256, 1024), BF16),
        compiler_params=params,
        cost_estimate=cost(4_300_000_000, 52_000_000),
        name="outputs",
    )(*tables, *x_pieces, blocks)

    outputs, cm, cp = barrier((outputs, cm, cp))
    c2a, c2b = along_y(cm[:8], 1), along_y(cp[8:], -1)

    near = (class_rows, cm, cp)
    near = near + tuple(other_core(piece) for piece in near)
    full = pl.BlockSpec((16, 32, 512), lambda i, *_: (0, 0, 0))
    part8 = pl.BlockSpec((8, 32, 512), lambda i, *_: (0, 0, 0))
    cot_groups = cot_all.reshape(16, 8, 32, 1024)

    def group(owner, chip_step, core_step):
        return lax.rem(lax.div(owner, 2) + chip_step, 4) * 2 + lax.rem(owner + core_step, 2)

    def near_group(i, pos):
        step = lax.rem(i, 3)
        chip_step = jnp.where(step == 1, 3, jnp.where(step == 2, 1, 0))
        return (0, group(pos[0], chip_step, lax.div(i, 3)), 0, 0)

    def far_group(i, pos, *_):
        return (0, group(pos[0], 2, i), 0, 0)

    total = jax.ShapeDtypeStruct((64, 8, 1024), F32)
    total_spec = pl.BlockSpec((64, 8, 1024), lambda i, *_: (0, 0, 0))
    near_grad = pl.pallas_call(
        near_grad_kernel,
        grid_spec=pltpu.PrefetchScalarGridSpec(
            num_scalar_prefetch=1,
            grid=(6,),
            in_specs=[full] * 6 + [pl.BlockSpec((16, 1, 32, 1024), near_group)],
            out_specs=total_spec,
            scratch_shapes=[pltpu.VMEM((512, 512), BF16)],
        ),
        out_shape=total,
        compiler_params=params,
        cost_estimate=cost(3_200_000_000, 32_000_000),
        name="near_weight_grad",
    )(pos, *near, cot_groups)

    sum_m, sum_p, near_grad = barrier((sum_m, sum_p, near_grad))
    context_sum = (keep[0] + rest[0] + sum_m + sum_p).astype(BF16)
    context_grad = exchange(context_sum)

    weight_grad = pl.pallas_call(
        functools.partial(far_grad_kernel, 1.0 / math.sqrt(4096)),
        grid_spec=pltpu.PrefetchScalarGridSpec(
            num_scalar_prefetch=4,
            grid=(2,),
            in_specs=[part8] * 4 + [pl.BlockSpec((16, 1, 32, 1024), far_group), total_spec],
            out_specs=pl.BlockSpec((1, 8, 34, 8, 128), lambda i, *_: (0, 0, 0, 0, 0)),
            scratch_shapes=[pltpu.VMEM((512, 512), BF16), pltpu.VMEM((64, 8, 1024), F32)],
        ),
        out_shape=jax.ShapeDtypeStruct((1, 8, 34, 8, 128), BF16),
        compiler_params=params,
        cost_estimate=cost(1_100_000_000, 25_000_000),
        name="far_weight_grad",
    )(*tables, c2a, c2b, other_core(c2a), other_core(c2b), cot_groups, near_grad)
    return (outputs, context_grad, weight_grad)


def solution(mesh):
    in_specs = (
        P(None, "mp", "seq"),
        P("mp", None, None, None, None),
        P(),
        P(),
        P(),
        P("seq", "mp"),
    )
    out_specs = (P("seq", "mp"), P(None, "mp", "seq"), P("mp", None, None, "seq", None))
    return jax.shard_map(
        on_device, mesh=mesh, in_specs=in_specs, out_specs=out_specs, check_vma=False
    )
```

```python
import functools
import math

import jax
import jax.numpy as jnp
from jax import lax
from jax.experimental import pallas as pl
from jax.experimental.pallas import tpu as pltpu
from jax.sharding import PartitionSpec as P

F32 = jnp.float32
BF16 = jnp.bfloat16
VMEM_LIMIT = 60 * 1024 * 1024


def build_panel(panel, blk_ref, rows_ref, cols_ref, live_ref, owner, j):
    panel[...] = jnp.zeros_like(panel)
    count = live_ref[owner, j]
    for k in range(34):

        def place(k=k):
            r = pl.multiple_of((rows_ref[owner, j, k] - 8 * j) * 128, 128)
            c = pl.multiple_of((cols_ref[owner, j, k] - 8 * owner) * 128, 128)
            panel[pl.ds(r, 128), pl.ds(c, 128)] = blk_ref[j, k]

        if k < 30:
            place()
        else:
            pl.when(k < count)(place)


def start_all(copies):
    for copy in copies:
        copy.start()


def wait_all(copies):
    for copy in copies:
        copy.wait()


def transpose_kernel(x_ref, o_ref):
    x = x_ref[...].reshape(512, 512).astype(F32)
    t = x.T.reshape(4, 16, 8, 512)
    for part in range(16):
        o_ref[part, pl.ds(0, 32)] = x_ref[part]
        o_ref[part, pl.ds(32, 32)] = t[:, part].reshape(32, 512).astype(BF16)


def partial_kernel(
    pos, rows, cols, live, cot, blk, keep, across, rest,
    lhs, blk_v, panel, keep_v, across_v, rest_v, cot_sem, blk_sem, out_sem,
):
    owner = pos[0]
    y = owner // 2
    core = owner % 2
    cot_copies = []
    for d in range(4):
        for side in range(2):
            who = core if side == 0 else 1 - core
            cot_copies.append(
                pltpu.make_async_copy(
                    cot.at[(y + d) % 4, who], lhs.at[pl.ds(side * 128 + d * 32, 32)], cot_sem.at[side * 4 + d]
                )
            )
    start_all(cot_copies)
    start_all([pltpu.make_async_copy(blk.at[0, j], blk_v.at[j], blk_sem.at[j]) for j in range(8)])
    wait_all(cot_copies)

    def out_copies(j):
        part = pl.ds(j * 2, 2)
        return (
            pltpu.make_async_copy(keep_v.at[:, part], keep.at[:, part], out_sem.at[j, 0]),
            pltpu.make_async_copy(across_v.at[part], across.at[part], out_sem.at[j, 1]),
            pltpu.make_async_copy(rest_v.at[:, part], rest.at[:, part], out_sem.at[j, 2]),
        )

    def step(j, carry):
        pltpu.make_async_copy(blk.at[0, j], blk_v.at[j], blk_sem.at[j]).wait()
        build_panel(panel, blk_v, rows, cols, live, owner, j)
        res = lax.dot_general(lhs[...], panel[...], (((1,), (1,)), ((), ())), preferred_element_type=F32)
        for half in range(2):
            lanes = slice(half * 512, half * 512 + 512)
            at = j * 2 + half
            for d in range(4):
                keep_v[d, at] = res[d * 32 : d * 32 + 32, lanes]
            rest_v[0, at] = res[128:160, lanes]
            rest_v[1, at] = res[160:192, lanes]
            across_v[at] = res[192:224, lanes]
            rest_v[2, at] = res[224:256, lanes]
        start_all(out_copies(j))
        return carry

    lax.fori_loop(0, 8, step, 0)
    for j in range(8):
        wait_all(out_copies(j))


def out_kernel(
    pos, rows, cols, live, a0, am, ap, a2a, a2b, b0, bm, bp, b2a, b2b, blk, out_ref,
    lhs, blk_v, panel, acc, x_sem, blk_sem,
):
    owner = pos[0]
    y = owner // 2
    core = owner % 2
    start_all([pltpu.make_async_copy(blk.at[0, j], blk_v.at[j], blk_sem.at[j]) for j in range(8)])
    x_copies = []
    for who, pieces in ((core, (a0, am, ap, a2a, a2b)), (1 - core, (b0, bm, bp, b2a, b2b))):
        places = (
            lhs.at[:, y, who],
            lhs.at[:, (y + 3) % 4, who],
            lhs.at[:, (y + 1) % 4, who],
            lhs.at[pl.ds(0, 8), (y + 2) % 4, who],
            lhs.at[pl.ds(8, 8), (y + 2) % 4, who],
        )
        for piece, place in zip(pieces, places):
            x_copies.append(pltpu.make_async_copy(piece, place, x_sem.at[len(x_copies)]))
    start_all(x_copies)
    acc[...] = jnp.zeros_like(acc)
    wait_all(x_copies)

    def step(j, carry):
        pltpu.make_async_copy(blk.at[0, j], blk_v.at[j], blk_sem.at[j]).wait()
        build_panel(panel, blk_v, rows, cols, live, owner, j)
        for half in range(2):
            acc[...] += jnp.dot(
                lhs[j * 2 + half].reshape(256, 512), panel[pl.ds(half * 512, 512)], preferred_element_type=F32
            )
        return carry

    lax.fori_loop(0, 8, step, 0)
    out_ref[...] = acc[...].astype(BF16)


def token_group(owner, chip_step, core_step):
    return ((owner // 2 + chip_step) % 4) * 2 + (owner + core_step) % 2


def near_grad_kernel(pos, a0, am, ap, b0, bm, bp, g, total, x_v, g_v, acc, x_sem, g_sem, out_sem):
    owner = pos[0]
    copies = []
    for at, piece in enumerate((a0, am, ap, b0, bm, bp)):
        group = token_group(owner, (0, 3, 1)[at % 3], at // 3)
        copies.append(
            (
                pltpu.make_async_copy(piece, x_v.at[at], x_sem.at[at]),
                pltpu.make_async_copy(g.at[:, group], g_v.at[at], g_sem.at[at]),
            )
        )
        start_all(copies[-1])
    for at in range(6):
        wait_all(copies[at])
        x, cot = x_v[at].reshape(512, 512), g_v[at].reshape(512, 1024)
        res = jnp.dot(x, cot, preferred_element_type=F32).reshape(64, 8, 1024)
        if at == 0:
            acc[...] = res
        else:
            acc[...] += res
    out = pltpu.make_async_copy(acc, total, out_sem.at[0])
    out.start()
    out.wait()


def far_grad_kernel(scale, pos, rows, cols, live, a2a, a2b, b2a, b2b, g, near, out_ref, x_v, g_v, acc, x_sem, g_sem, near_sem):
    owner = pos[0]
    near_copy = pltpu.make_async_copy(near, acc, near_sem.at[0])
    near_copy.start()
    copies = []
    for at, (first, second) in enumerate(((a2a, a2b), (b2a, b2b))):
        group = token_group(owner, 2, at)
        copies.append(
            (
                pltpu.make_async_copy(first, x_v.at[at, pl.ds(0, 8)], x_sem.at[at, 0]),
                pltpu.make_async_copy(second, x_v.at[at, pl.ds(8, 8)], x_sem.at[at, 1]),
                pltpu.make_async_copy(g.at[:, group], g_v.at[at], g_sem.at[at]),
            )
        )
        start_all(copies[-1])
    near_copy.wait()
    for at in range(2):
        wait_all(copies[at])
        x, cot = x_v[at].reshape(512, 512), g_v[at].reshape(512, 1024)
        acc[...] += jnp.dot(x, cot, preferred_element_type=F32).reshape(64, 8, 1024)

    def pick(j, carry):
        count = live[owner, j]
        for k in range(34):
            r = rows[owner, j, k]
            c = pl.multiple_of((cols[owner, j, k] - 8 * owner) * 128, 128)
            tile = acc[r, :, pl.ds(c, 128)] * scale
            if k >= 30:
                tile = jnp.where(k < count, tile, 0.0)
            out_ref[0, j, k] = tile.astype(BF16)
        return carry

    lax.fori_loop(0, 8, pick, 0)


def on_device(context, blocks, row_blocks, col_blocks, live_counts, cotangent):
    owner = lax.axis_index("mp")
    pos = owner.astype(jnp.int32).reshape(1)
    tables = (pos, row_blocks, col_blocks, live_counts)
    params = pltpu.CompilerParams(vmem_limit_bytes=VMEM_LIMIT)
    barrier = lax.optimization_barrier

    def cost(flops, size):
        return pl.CostEstimate(flops=flops, bytes_accessed=size, transcendentals=0)

    def along_y(x, step):
        return lax.ppermute(x, "mp", [(i, (i + 2 * step) % 8) for i in range(8)])

    def other_core(x):
        return lax.ppermute(x, "mp", [(i, i ^ 1) for i in range(8)])

    def exchange(x):
        return lax.all_to_all(x, "seq", split_axis=0, concat_axis=0, tiled=True)

    cot_all = lax.all_gather(cotangent, "seq", axis=0, tiled=True)

    both = pl.pallas_call(
        transpose_kernel,
        out_shape=jax.ShapeDtypeStruct((16, 64, 512), BF16),
        compiler_params=params,
        name="feature_rows",
    )(context)
    both, cot_own = barrier((both, cotangent))
    both = exchange(both)
    tokens, class_rows = both[:, :32], both[:, 32:]

    scalars = [pl.BlockSpec(memory_space=pltpu.SMEM)] * 4
    anywhere = pl.BlockSpec(memory_space=pl.ANY)
    keep, across, rest = pl.pallas_call(
        partial_kernel,
        in_specs=scalars + [anywhere] * 2,
        out_specs=[anywhere] * 3,
        out_shape=[
            jax.ShapeDtypeStruct((4, 16, 32, 512), F32),
            jax.ShapeDtypeStruct((16, 32, 512), F32),
            jax.ShapeDtypeStruct((3, 16, 32, 512), F32),
        ],
        scratch_shapes=[
            pltpu.VMEM((256, 1024), BF16),
            pltpu.VMEM((8, 34, 128, 128), BF16),
            pltpu.VMEM((1024, 1024), BF16),
            pltpu.VMEM((4, 16, 32, 512), F32),
            pltpu.VMEM((16, 32, 512), F32),
            pltpu.VMEM((3, 16, 32, 512), F32),
            pltpu.SemaphoreType.DMA((8,)),
            pltpu.SemaphoreType.DMA((8,)),
            pltpu.SemaphoreType.DMA((8, 3)),
        ],
        compiler_params=params,
        cost_estimate=cost(4_300_000_000, 40_000_000),
        name="partial_context_grad",
    )(*tables, cot_own.reshape(4, 2, 32, 1024), blocks)
    across = other_core(across)

    xm, xp = along_y(tokens, 1), along_y(tokens, -1)
    rest, _ = barrier((rest, tokens))
    rest = other_core(rest)

    q2a, q2b, xm, xp = barrier((keep[2, :8] + across[:8], keep[2, 8:] + across[8:], xm, xp))
    x2a, x2b = along_y(xm[:8], 1), along_y(xp[8:], -1)
    x2a, x2b, q2a, q2b, class_rows = barrier((x2a, x2b, q2a, q2b, class_rows))
    from_a, from_b = along_y(q2a, 1), along_y(q2b, -1)
    own = (tokens, xm, xp, x2a, x2b)
    x_pieces = own + tuple(other_core(piece) for piece in own)

    cm, cp = along_y(class_rows, 1), along_y(class_rows, -1)

    outputs = pl.pallas_call(
        out_kernel,
        in_specs=scalars + [anywhere] * 11,
        out_shape=jax.ShapeDtypeStruct((256, 1024), BF16),
        scratch_shapes=[
            pltpu.VMEM((16, 4, 2, 32, 512), BF16),
            pltpu.VMEM((8, 34, 128, 128), BF16),
            pltpu.VMEM((1024, 1024), BF16),
            pltpu.VMEM((256, 1024), F32),
            pltpu.SemaphoreType.DMA((10,)),
            pltpu.SemaphoreType.DMA((8,)),
        ],
        compiler_params=params,
        cost_estimate=cost(4_300_000_000, 40_000_000),
        name="outputs",
    )(*tables, *x_pieces, blocks)

    outputs, cm, cp, from_a, from_b = barrier((outputs, cm, cp, from_a, from_b))
    q1 = jnp.concatenate([keep[1, :8] + rest[1, :8] + from_a, keep[1, 8:] + rest[1, 8:]], axis=0)
    q3 = jnp.concatenate([keep[3, :8] + rest[2, :8], keep[3, 8:] + rest[2, 8:] + from_b], axis=0)
    sum_m, sum_p = along_y(q1, 1), along_y(q3, -1)
    c2a, c2b = along_y(cm[:8], 1), along_y(cp[8:], -1)

    near = (class_rows, cm, cp)
    near = near + tuple(other_core(piece) for piece in near)
    cot_groups = cot_all.reshape(16, 8, 32, 1024)
    near_grad = pl.pallas_call(
        near_grad_kernel,
        in_specs=scalars[:1] + [anywhere] * 7,
        out_specs=anywhere,
        out_shape=jax.ShapeDtypeStruct((64, 8, 1024), F32),
        scratch_shapes=[
            pltpu.VMEM((6, 16, 32, 512), BF16),
            pltpu.VMEM((6, 16, 32, 1024), BF16),
            pltpu.VMEM((64, 8, 1024), F32),
            pltpu.SemaphoreType.DMA((6,)),
            pltpu.SemaphoreType.DMA((6,)),
            pltpu.SemaphoreType.DMA((1,)),
        ],
        compiler_params=params,
        cost_estimate=cost(3_200_000_000, 25_000_000),
        name="near_weight_grad",
    )(pos, *near, cot_groups)

    sum_m, sum_p, near_grad = barrier((sum_m, sum_p, near_grad))
    context_sum = (keep[0] + rest[0] + sum_m + sum_p).astype(BF16)
    context_grad = exchange(context_sum)

    weight_grad = pl.pallas_call(
        functools.partial(far_grad_kernel, 1.0 / math.sqrt(4096)),
        in_specs=scalars + [anywhere] * 6,
        out_shape=jax.ShapeDtypeStruct((1, 8, 34, 8, 128), BF16),
        scratch_shapes=[
            pltpu.VMEM((2, 16, 32, 512), BF16),
            pltpu.VMEM((2, 16, 32, 1024), BF16),
            pltpu.VMEM((64, 8, 1024), F32),
            pltpu.SemaphoreType.DMA((2, 2)),
            pltpu.SemaphoreType.DMA((2,)),
            pltpu.SemaphoreType.DMA((1,)),
        ],
        compiler_params=params,
        cost_estimate=cost(1_100_000_000, 18_000_000),
        name="far_weight_grad",
    )(*tables, c2a, c2b, other_core(c2a), other_core(c2b), cot_groups, near_grad)
    return (outputs, context_grad, weight_grad)


def solution(mesh):
    in_specs = (
        P(None, "mp", "seq"),
        P("mp", None, None, None, None),
        P(),
        P(),
        P(),
        P("seq", "mp"),
    )
    out_specs = (P("seq", "mp"), P(None, "mp", "seq"), P("mp", None, None, "seq", None))
    return jax.shard_map(
        on_device, mesh=mesh, in_specs=in_specs, out_specs=out_specs, check_vma=False
    )
```

```python
import functools
import math

import jax
import jax.numpy as jnp
from jax import lax
from jax.experimental import pallas as pl
from jax.experimental.pallas import tpu as pltpu
from jax.sharding import PartitionSpec as P

F32 = jnp.float32
BF16 = jnp.bfloat16
VMEM_LIMIT = 60 * 1024 * 1024


def build_panel(panel, blk_ref, rows_ref, cols_ref, live_ref, owner, j):
    panel[...] = jnp.zeros_like(panel)
    count = live_ref[owner, j]
    for k in range(34):
        r = pl.multiple_of((rows_ref[owner, j, k] - 8 * j) * 128, 128)
        c = pl.multiple_of((cols_ref[owner, j, k] - 8 * owner) * 128, 128)
        block = blk_ref[k]
        if k >= 30:
            block = jnp.where(k < count, block, jnp.zeros_like(block))
        panel[pl.ds(r, 128), pl.ds(c, 128)] = block


def start_all(copies):
    for copy in copies:
        copy.start()


def wait_all(copies):
    for copy in copies:
        copy.wait()


def transpose_kernel(x_ref, o_ref):
    x = x_ref[...].reshape(512, 512).astype(F32)
    t = x.T.reshape(4, 16, 8, 512)
    for part in range(16):
        o_ref[part, pl.ds(0, 32)] = x_ref[part]
        o_ref[part, pl.ds(32, 32)] = t[:, part].reshape(32, 512).astype(BF16)


def partial_kernel(pos, rows, cols, live, cot, blk, keep, across, rest, dense, *scratch):
    lhs, keep_v, across_v, rest_v, cot_sem, blk_sem, out_sem = scratch[:7]
    blk_v, panels = scratch[7:15], scratch[15:23]
    owner = pos[0]
    y = owner // 2
    core = owner % 2
    cot_copies = []
    for d in range(4):
        for side in range(2):
            who = core if side == 0 else 1 - core
            cot_copies.append(
                pltpu.make_async_copy(
                    cot.at[(y + d) % 4, who], lhs.at[pl.ds(side * 128 + d * 32, 32)], cot_sem.at[side * 4 + d]
                )
            )
    blk_copies = [pltpu.make_async_copy(blk.at[0, j], blk_v[j], blk_sem.at[j]) for j in range(8)]
    start_all(cot_copies)
    start_all(blk_copies)

    out_copies = []
    blk_copies[0].wait()
    build_panel(panels[0], blk_v[0], rows, cols, live, owner, 0)
    wait_all(cot_copies)
    for j in range(8):
        if j < 7:
            blk_copies[j + 1].wait()
        res = lax.dot_general(lhs[...], panels[j][...], (((1,), (1,)), ((), ())), preferred_element_type=F32)
        if j < 7:
            build_panel(panels[j + 1], blk_v[j + 1], rows, cols, live, owner, j + 1)
        for half in range(2):
            lanes = slice(half * 512, half * 512 + 512)
            at = j * 2 + half
            for d in range(4):
                keep_v[d, at] = res[d * 32 : d * 32 + 32, lanes]
            rest_v[0, at] = res[128:160, lanes]
            rest_v[1, at] = res[160:192, lanes]
            across_v[at] = res[192:224, lanes]
            rest_v[2, at] = res[224:256, lanes]
        part = pl.ds(j * 2, 2)
        step_copies = [
            pltpu.make_async_copy(panels[j], dense.at[j], out_sem.at[j, 0]),
            pltpu.make_async_copy(keep_v.at[:, part], keep.at[:, part], out_sem.at[j, 1]),
            pltpu.make_async_copy(across_v.at[part], across.at[part], out_sem.at[j, 2]),
            pltpu.make_async_copy(rest_v.at[:, part], rest.at[:, part], out_sem.at[j, 3]),
        ]
        start_all(step_copies)
        out_copies += step_copies
    wait_all(out_copies)


def out_kernel(pos, a0, am, ap, a2a, a2b, b0, bm, bp, b2a, b2b, dense, out_ref, lhs, panels, acc, x_sem, dense_sem):
    owner = pos[0]
    y = owner // 2
    core = owner % 2
    x_copies = []
    for who, pieces in ((core, (a0, am, ap, a2a, a2b)), (1 - core, (b0, bm, bp, b2a, b2b))):
        places = (
            lhs.at[:, y, who],
            lhs.at[:, (y + 3) % 4, who],
            lhs.at[:, (y + 1) % 4, who],
            lhs.at[pl.ds(0, 8), (y + 2) % 4, who],
            lhs.at[pl.ds(8, 8), (y + 2) % 4, who],
        )
        for piece, place in zip(pieces, places):
            x_copies.append(pltpu.make_async_copy(piece, place, x_sem.at[len(x_copies)]))
    dense_copies = [pltpu.make_async_copy(dense.at[j], panels.at[j], dense_sem.at[j]) for j in range(8)]
    start_all(x_copies)
    start_all(dense_copies)
    wait_all(x_copies)
    for j in range(8):
        dense_copies[j].wait()
        first = jnp.dot(lhs[j * 2].reshape(256, 512), panels[j, :512], preferred_element_type=F32)
        second = jnp.dot(lhs[j * 2 + 1].reshape(256, 512), panels[j, 512:], preferred_element_type=F32)
        if j == 0:
            acc[...] = first + second
        elif j < 7:
            acc[...] += first + second
        else:
            out_ref[...] = (acc[...] + first + second).astype(BF16)


def token_group(owner, chip_step, core_step):
    return ((owner // 2 + chip_step) % 4) * 2 + (owner + core_step) % 2


def near_grad_kernel(pos, a0, am, ap, b0, bm, bp, g, total, x_v, g_v, acc, x_sem, g_sem, out_sem):
    owner = pos[0]
    copies = []
    for at, piece in enumerate((a0, am, ap, b0, bm, bp)):
        group = token_group(owner, (0, 3, 1)[at % 3], at // 3)
        copies.append(
            (
                pltpu.make_async_copy(piece, x_v.at[at], x_sem.at[at]),
                pltpu.make_async_copy(g.at[:, group], g_v.at[at], g_sem.at[at]),
            )
        )
        start_all(copies[-1])
    for at in range(6):
        wait_all(copies[at])
        x, cot = x_v[at].reshape(512, 512), g_v[at].reshape(512, 1024)
        res = jnp.dot(x, cot, preferred_element_type=F32).reshape(64, 8, 1024)
        if at == 0:
            acc[...] = res
        else:
            acc[...] += res
    out = pltpu.make_async_copy(acc, total, out_sem.at[0])
    out.start()
    out.wait()


def far_grad_kernel(scale, pos, rows, cols, live, a2a, a2b, b2a, b2b, g, near, out_ref, x_v, g_v, acc, x_sem, g_sem, near_sem):
    owner = pos[0]
    near_copy = pltpu.make_async_copy(near, acc, near_sem.at[0])
    near_copy.start()
    copies = []
    for at, (first, second) in enumerate(((a2a, a2b), (b2a, b2b))):
        group = token_group(owner, 2, at)
        copies.append(
            (
                pltpu.make_async_copy(first, x_v.at[at, pl.ds(0, 8)], x_sem.at[at, 0]),
                pltpu.make_async_copy(second, x_v.at[at, pl.ds(8, 8)], x_sem.at[at, 1]),
                pltpu.make_async_copy(g.at[:, group], g_v.at[at], g_sem.at[at]),
            )
        )
        start_all(copies[-1])
    near_copy.wait()
    for at in range(2):
        wait_all(copies[at])
        x, cot = x_v[at].reshape(512, 512), g_v[at].reshape(512, 1024)
        acc[...] += jnp.dot(x, cot, preferred_element_type=F32).reshape(64, 8, 1024)

    def pick(j, carry):
        count = live[owner, j]
        for k in range(34):
            r = rows[owner, j, k]
            c = pl.multiple_of((cols[owner, j, k] - 8 * owner) * 128, 128)
            tile = acc[r, :, pl.ds(c, 128)] * scale
            if k >= 30:
                tile = jnp.where(k < count, tile, 0.0)
            out_ref[0, j, k] = tile.astype(BF16)
        return carry

    lax.fori_loop(0, 8, pick, 0)


def on_device(context, blocks, row_blocks, col_blocks, live_counts, cotangent):
    owner = lax.axis_index("mp")
    pos = owner.astype(jnp.int32).reshape(1)
    tables = (pos, row_blocks, col_blocks, live_counts)
    params = pltpu.CompilerParams(vmem_limit_bytes=VMEM_LIMIT)
    barrier = lax.optimization_barrier

    def cost(flops, size):
        return pl.CostEstimate(flops=flops, bytes_accessed=size, transcendentals=0)

    def along_y(x, step):
        return lax.ppermute(x, "mp", [(i, (i + 2 * step) % 8) for i in range(8)])

    def other_core(x):
        return lax.ppermute(x, "mp", [(i, i ^ 1) for i in range(8)])

    def exchange(x):
        return lax.all_to_all(x, "seq", split_axis=0, concat_axis=0, tiled=True)

    cot_all = lax.all_gather(cotangent, "seq", axis=0, tiled=True)

    both = pl.pallas_call(
        transpose_kernel,
        out_shape=jax.ShapeDtypeStruct((16, 64, 512), BF16),
        compiler_params=params,
        name="feature_rows",
    )(context)
    both, cot_own = barrier((both, cotangent))
    both = exchange(both)
    tokens, class_rows = both[:, :32], both[:, 32:]

    scalars = [pl.BlockSpec(memory_space=pltpu.SMEM)] * 4
    anywhere = pl.BlockSpec(memory_space=pl.ANY)
    keep, across, rest, dense = pl.pallas_call(
        partial_kernel,
        in_specs=scalars + [anywhere] * 2,
        out_specs=[anywhere] * 4,
        out_shape=[
            jax.ShapeDtypeStruct((4, 16, 32, 512), F32),
            jax.ShapeDtypeStruct((16, 32, 512), F32),
            jax.ShapeDtypeStruct((3, 16, 32, 512), F32),
            jax.ShapeDtypeStruct((8, 1024, 1024), BF16),
        ],
        scratch_shapes=[
            pltpu.VMEM((256, 1024), BF16),
            pltpu.VMEM((4, 16, 32, 512), F32),
            pltpu.VMEM((16, 32, 512), F32),
            pltpu.VMEM((3, 16, 32, 512), F32),
            pltpu.SemaphoreType.DMA((8,)),
            pltpu.SemaphoreType.DMA((8,)),
            pltpu.SemaphoreType.DMA((8, 4)),
        ]
        + [pltpu.VMEM((34, 128, 128), BF16)] * 8
        + [pltpu.VMEM((1024, 1024), BF16)] * 8,
        compiler_params=params,
        cost_estimate=cost(4_300_000_000, 45_000_000),
        name="partial_context_grad",
    )(*tables, cot_own.reshape(4, 2, 32, 1024), blocks)
    across = other_core(across)

    q2a, q2b = keep[2, :8] + across[:8], keep[2, 8:] + across[8:]
    q2a, q2b, tokens, rest = barrier((q2a, q2b, tokens, rest))
    from_a, from_b = along_y(q2a, 1), along_y(q2b, -1)
    xm, xp = along_y(tokens, 1), along_y(tokens, -1)
    rest = other_core(rest)
    x2a, x2b = along_y(xm[:8], 1), along_y(xp[8:], -1)
    x2a, x2b, class_rows = barrier((x2a, x2b, class_rows))
    own = (tokens, xm, xp, x2a, x2b)
    x_pieces = own + tuple(other_core(piece) for piece in own)

    cm, cp = along_y(class_rows, 1), along_y(class_rows, -1)

    q1 = jnp.concatenate([keep[1, :8] + rest[1, :8] + from_a, keep[1, 8:] + rest[1, 8:]], axis=0)
    q3 = jnp.concatenate([keep[3, :8] + rest[2, :8], keep[3, 8:] + rest[2, 8:] + from_b], axis=0)
    q1, q3, x_pieces = barrier((q1, q3, x_pieces))
    sum_m, sum_p = along_y(q1, 1), along_y(q3, -1)

    outputs = pl.pallas_call(
        out_kernel,
        in_specs=scalars[:1] + [anywhere] * 11,
        out_shape=jax.ShapeDtypeStruct((256, 1024), BF16),
        scratch_shapes=[
            pltpu.VMEM((16, 4, 2, 32, 512), BF16),
            pltpu.VMEM((8, 1024, 1024), BF16),
            pltpu.VMEM((256, 1024), F32),
            pltpu.SemaphoreType.DMA((10,)),
            pltpu.SemaphoreType.DMA((8,)),
        ],
        compiler_params=params,
        cost_estimate=cost(4_300_000_000, 30_000_000),
        name="outputs",
    )(pos, *x_pieces, dense)

    outputs, cm, cp = barrier((outputs, cm, cp))
    c2a, c2b = along_y(cm[:8], 1), along_y(cp[8:], -1)

    near = (class_rows, cm, cp)
    near = near + tuple(other_core(piece) for piece in near)
    cot_groups = cot_all.reshape(16, 8, 32, 1024)
    near_grad = pl.pallas_call(
        near_grad_kernel,
        in_specs=scalars[:1] + [anywhere] * 7,
        out_specs=anywhere,
        out_shape=jax.ShapeDtypeStruct((64, 8, 1024), F32),
        scratch_shapes=[
            pltpu.VMEM((6, 16, 32, 512), BF16),
            pltpu.VMEM((6, 16, 32, 1024), BF16),
            pltpu.VMEM((64, 8, 1024), F32),
            pltpu.SemaphoreType.DMA((6,)),
            pltpu.SemaphoreType.DMA((6,)),
            pltpu.SemaphoreType.DMA((1,)),
        ],
        compiler_params=params,
        cost_estimate=cost(3_200_000_000, 25_000_000),
        name="near_weight_grad",
    )(pos, *near, cot_groups)

    sum_m, sum_p, near_grad = barrier((sum_m, sum_p, near_grad))
    context_sum = (keep[0] + rest[0] + sum_m + sum_p).astype(BF16)
    context_grad = exchange(context_sum)

    weight_grad = pl.pallas_call(
        functools.partial(far_grad_kernel, 1.0 / math.sqrt(4096)),
        in_specs=scalars + [anywhere] * 6,
        out_shape=jax.ShapeDtypeStruct((1, 8, 34, 8, 128), BF16),
        scratch_shapes=[
            pltpu.VMEM((2, 16, 32, 512), BF16),
            pltpu.VMEM((2, 16, 32, 1024), BF16),
            pltpu.VMEM((64, 8, 1024), F32),
            pltpu.SemaphoreType.DMA((2, 2)),
            pltpu.SemaphoreType.DMA((2,)),
            pltpu.SemaphoreType.DMA((1,)),
        ],
        compiler_params=params,
        cost_estimate=cost(1_100_000_000, 18_000_000),
        name="far_weight_grad",
    )(*tables, c2a, c2b, other_core(c2a), other_core(c2b), cot_groups, near_grad)
    return (outputs, context_grad, weight_grad)


def solution(mesh):
    in_specs = (
        P(None, "mp", "seq"),
        P("mp", None, None, None, None),
        P(),
        P(),
        P(),
        P("seq", "mp"),
    )
    out_specs = (P("seq", "mp"), P(None, "mp", "seq"), P("mp", None, None, "seq", None))
    return jax.shard_map(
        on_device, mesh=mesh, in_specs=in_specs, out_specs=out_specs, check_vma=False
    )
```

```python
import functools
import math

import jax
import jax.numpy as jnp
from jax import lax
from jax.experimental import pallas as pl
from jax.experimental.pallas import tpu as pltpu
from jax.sharding import PartitionSpec as P

F32 = jnp.float32
BF16 = jnp.bfloat16
VMEM_LIMIT = 60 * 1024 * 1024


def build_panel(panel, blk_ref, rows_ref, cols_ref, live_ref, owner, j):
    panel[...] = jnp.zeros_like(panel)
    count = live_ref[owner, j]
    for k in range(34):
        r = pl.multiple_of((rows_ref[owner, j, k] - 8 * j) * 128, 128)
        c = pl.multiple_of((cols_ref[owner, j, k] - 8 * owner) * 128, 128)
        block = blk_ref[k]
        if k >= 30:
            block = jnp.where(k < count, block, jnp.zeros_like(block))
        panel[pl.ds(r, 128), pl.ds(c, 128)] = block


def start_all(copies):
    for copy in copies:
        copy.start()


def wait_all(copies):
    for copy in copies:
        copy.wait()


def transpose_kernel(x_ref, o_ref):
    x = x_ref[...].reshape(512, 512).astype(F32)
    t = x.T.reshape(4, 16, 8, 512)
    for part in range(16):
        o_ref[part, pl.ds(0, 32)] = x_ref[part]
        o_ref[part, pl.ds(32, 32)] = t[:, part].reshape(32, 512).astype(BF16)


def partial_kernel(pos, rows, cols, live, cot, blk, keep, across, rest, *scratch):
    lhs, keep_v, across_v, rest_v, cot_sem, blk_sem, out_sem = scratch[:7]
    blk_v, panels = scratch[7:15], scratch[15:23]
    owner = pos[0]
    y = owner // 2
    core = owner % 2
    cot_copies = []
    for d in range(4):
        for side in range(2):
            who = core if side == 0 else 1 - core
            cot_copies.append(
                pltpu.make_async_copy(
                    cot.at[(y + d) % 4, who], lhs.at[pl.ds(side * 128 + d * 32, 32)], cot_sem.at[side * 4 + d]
                )
            )
    blk_copies = [pltpu.make_async_copy(blk.at[0, j], blk_v[j], blk_sem.at[j]) for j in range(8)]
    start_all(cot_copies)
    start_all(blk_copies)

    out_copies = []
    blk_copies[0].wait()
    build_panel(panels[0], blk_v[0], rows, cols, live, owner, 0)
    wait_all(cot_copies)
    for j in range(8):
        if j < 7:
            blk_copies[j + 1].wait()
        res = lax.dot_general(lhs[...], panels[j][...], (((1,), (1,)), ((), ())), preferred_element_type=F32)
        if j < 7:
            build_panel(panels[j + 1], blk_v[j + 1], rows, cols, live, owner, j + 1)
        for half in range(2):
            lanes = slice(half * 512, half * 512 + 512)
            at = j * 2 + half
            for d in range(4):
                keep_v[d, at] = res[d * 32 : d * 32 + 32, lanes]
            rest_v[0, at] = res[128:160, lanes]
            rest_v[1, at] = res[160:192, lanes]
            across_v[at] = res[192:224, lanes]
            rest_v[2, at] = res[224:256, lanes]
        part = pl.ds(j * 2, 2)
        step_copies = [
            pltpu.make_async_copy(keep_v.at[:, part], keep.at[:, part], out_sem.at[j, 0]),
            pltpu.make_async_copy(across_v.at[part], across.at[part], out_sem.at[j, 1]),
            pltpu.make_async_copy(rest_v.at[:, part], rest.at[:, part], out_sem.at[j, 2]),
        ]
        start_all(step_copies)
        out_copies += step_copies
    wait_all(out_copies)


def dense_kernel(pos, rows, cols, live, blk, dense, blk_v, panels, blk_sem, out_sem):
    blk_copies = [pltpu.make_async_copy(blk.at[0, j], blk_v.at[j], blk_sem.at[j]) for j in range(8)]
    out_copies = [pltpu.make_async_copy(panels.at[j], dense.at[j], out_sem.at[j]) for j in range(8)]
    start_all(blk_copies)
    for j in range(8):
        blk_copies[j].wait()
        build_panel(panels.at[j], blk_v.at[j], rows, cols, live, pos[0], j)
        out_copies[j].start()
    wait_all(out_copies)


def out_kernel(pos, a0, am, ap, a2a, a2b, b0, bm, bp, b2a, b2b, dense, out_ref, lhs, panels, acc, x_sem, dense_sem):
    owner = pos[0]
    y = owner // 2
    core = owner % 2
    x_copies = []
    for who, pieces in ((core, (a0, am, ap, a2a, a2b)), (1 - core, (b0, bm, bp, b2a, b2b))):
        places = (
            lhs.at[:, y, who],
            lhs.at[:, (y + 3) % 4, who],
            lhs.at[:, (y + 1) % 4, who],
            lhs.at[pl.ds(0, 8), (y + 2) % 4, who],
            lhs.at[pl.ds(8, 8), (y + 2) % 4, who],
        )
        for piece, place in zip(pieces, places):
            x_copies.append(pltpu.make_async_copy(piece, place, x_sem.at[len(x_copies)]))
    dense_copies = [pltpu.make_async_copy(dense.at[j], panels.at[j], dense_sem.at[j]) for j in range(8)]
    start_all(x_copies)
    start_all(dense_copies)
    wait_all(x_copies)
    for j in range(8):
        dense_copies[j].wait()
        first = jnp.dot(lhs[j * 2].reshape(256, 512), panels[j, :512], preferred_element_type=F32)
        second = jnp.dot(lhs[j * 2 + 1].reshape(256, 512), panels[j, 512:], preferred_element_type=F32)
        if j == 0:
            acc[...] = first + second
        elif j < 7:
            acc[...] += first + second
        else:
            out_ref[...] = (acc[...] + first + second).astype(BF16)


def token_group(owner, chip_step, core_step):
    return ((owner // 2 + chip_step) % 4) * 2 + (owner + core_step) % 2


def near_grad_kernel(pos, a0, am, ap, b0, bm, bp, g, total, x_v, g_v, acc, x_sem, g_sem, out_sem):
    owner = pos[0]
    copies = []
    for at, piece in enumerate((a0, am, ap, b0, bm, bp)):
        group = token_group(owner, (0, 3, 1)[at % 3], at // 3)
        copies.append(
            (
                pltpu.make_async_copy(piece, x_v.at[at], x_sem.at[at]),
                pltpu.make_async_copy(g.at[:, group], g_v.at[at], g_sem.at[at]),
            )
        )
        start_all(copies[-1])
    for at in range(6):
        wait_all(copies[at])
        x, cot = x_v[at].reshape(512, 512), g_v[at].reshape(512, 1024)
        res = jnp.dot(x, cot, preferred_element_type=F32).reshape(64, 8, 1024)
        if at == 0:
            acc[...] = res
        else:
            acc[...] += res
    out = pltpu.make_async_copy(acc, total, out_sem.at[0])
    out.start()
    out.wait()


def far_grad_kernel(scale, pos, rows, cols, live, a2a, a2b, b2a, b2b, g, near, out_ref, x_v, g_v, acc, x_sem, g_sem, near_sem):
    owner = pos[0]
    near_copy = pltpu.make_async_copy(near, acc, near_sem.at[0])
    near_copy.start()
    copies = []
    for at, (first, second) in enumerate(((a2a, a2b), (b2a, b2b))):
        group = token_group(owner, 2, at)
        copies.append(
            (
                pltpu.make_async_copy(first, x_v.at[at, pl.ds(0, 8)], x_sem.at[at, 0]),
                pltpu.make_async_copy(second, x_v.at[at, pl.ds(8, 8)], x_sem.at[at, 1]),
                pltpu.make_async_copy(g.at[:, group], g_v.at[at], g_sem.at[at]),
            )
        )
        start_all(copies[-1])
    near_copy.wait()
    for at in range(2):
        wait_all(copies[at])
        x, cot = x_v[at].reshape(512, 512), g_v[at].reshape(512, 1024)
        acc[...] += jnp.dot(x, cot, preferred_element_type=F32).reshape(64, 8, 1024)

    def pick(j, carry):
        count = live[owner, j]
        for k in range(34):
            r = rows[owner, j, k]
            c = pl.multiple_of((cols[owner, j, k] - 8 * owner) * 128, 128)
            tile = acc[r, :, pl.ds(c, 128)] * scale
            if k >= 30:
                tile = jnp.where(k < count, tile, 0.0)
            out_ref[0, j, k] = tile.astype(BF16)
        return carry

    lax.fori_loop(0, 8, pick, 0)


def on_device(context, blocks, row_blocks, col_blocks, live_counts, cotangent):
    owner = lax.axis_index("mp")
    pos = owner.astype(jnp.int32).reshape(1)
    tables = (pos, row_blocks, col_blocks, live_counts)
    params = pltpu.CompilerParams(vmem_limit_bytes=VMEM_LIMIT)
    barrier = lax.optimization_barrier

    def cost(flops, size):
        return pl.CostEstimate(flops=flops, bytes_accessed=size, transcendentals=0)

    def along_y(x, step):
        return lax.ppermute(x, "mp", [(i, (i + 2 * step) % 8) for i in range(8)])

    def other_core(x):
        return lax.ppermute(x, "mp", [(i, i ^ 1) for i in range(8)])

    def exchange(x):
        return lax.all_to_all(x, "seq", split_axis=0, concat_axis=0, tiled=True)

    cot_all = lax.all_gather(cotangent, "seq", axis=0, tiled=True)

    both = pl.pallas_call(
        transpose_kernel,
        out_shape=jax.ShapeDtypeStruct((16, 64, 512), BF16),
        compiler_params=params,
        name="feature_rows",
    )(context)
    both, cot_own = barrier((both, cotangent))
    both = exchange(both)
    tokens, class_rows = both[:, :32], both[:, 32:]

    scalars = [pl.BlockSpec(memory_space=pltpu.SMEM)] * 4
    anywhere = pl.BlockSpec(memory_space=pl.ANY)
    keep, across, rest = pl.pallas_call(
        partial_kernel,
        in_specs=scalars + [anywhere] * 2,
        out_specs=[anywhere] * 3,
        out_shape=[
            jax.ShapeDtypeStruct((4, 16, 32, 512), F32),
            jax.ShapeDtypeStruct((16, 32, 512), F32),
            jax.ShapeDtypeStruct((3, 16, 32, 512), F32),
        ],
        scratch_shapes=[
            pltpu.VMEM((256, 1024), BF16),
            pltpu.VMEM((4, 16, 32, 512), F32),
            pltpu.VMEM((16, 32, 512), F32),
            pltpu.VMEM((3, 16, 32, 512), F32),
            pltpu.SemaphoreType.DMA((8,)),
            pltpu.SemaphoreType.DMA((8,)),
            pltpu.SemaphoreType.DMA((8, 3)),
        ]
        + [pltpu.VMEM((34, 128, 128), BF16)] * 8
        + [pltpu.VMEM((1024, 1024), BF16)] * 8,
        compiler_params=params,
        cost_estimate=cost(4_300_000_000, 45_000_000),
        name="partial_context_grad",
    )(*tables, cot_own.reshape(4, 2, 32, 1024), blocks)
    across = other_core(across)

    q2a, q2b = keep[2, :8] + across[:8], keep[2, 8:] + across[8:]
    q2a, q2b, tokens, rest = barrier((q2a, q2b, tokens, rest))
    from_a, from_b = along_y(q2a, 1), along_y(q2b, -1)
    xm, xp = along_y(tokens, 1), along_y(tokens, -1)
    rest = other_core(rest)
    xma, xpb, blk_later = barrier((xm[:8], xp[8:], blocks))
    x2a, x2b = along_y(xma, 1), along_y(xpb, -1)
    dense = pl.pallas_call(
        dense_kernel,
        in_specs=scalars + [anywhere],
        out_specs=anywhere,
        out_shape=jax.ShapeDtypeStruct((8, 1024, 1024), BF16),
        scratch_shapes=[
            pltpu.VMEM((8, 34, 128, 128), BF16),
            pltpu.VMEM((8, 1024, 1024), BF16),
            pltpu.SemaphoreType.DMA((8,)),
            pltpu.SemaphoreType.DMA((8,)),
        ],
        compiler_params=params,
        cost_estimate=cost(0, 30_000_000),
        name="dense_panels",
    )(*tables, blk_later)
    x2a, x2b, class_rows = barrier((x2a, x2b, class_rows))
    own = (tokens, xm, xp, x2a, x2b)
    x_pieces = own + tuple(other_core(piece) for piece in own)

    cm, cp = along_y(class_rows, 1), along_y(class_rows, -1)

    q1 = jnp.concatenate([keep[1, :8] + rest[1, :8] + from_a, keep[1, 8:] + rest[1, 8:]], axis=0)
    q3 = jnp.concatenate([keep[3, :8] + rest[2, :8], keep[3, 8:] + rest[2, 8:] + from_b], axis=0)
    q1, q3, x_pieces = barrier((q1, q3, x_pieces))
    sum_m, sum_p = along_y(q1, 1), along_y(q3, -1)

    outputs = pl.pallas_call(
        out_kernel,
        in_specs=scalars[:1] + [anywhere] * 11,
        out_shape=jax.ShapeDtypeStruct((256, 1024), BF16),
        scratch_shapes=[
            pltpu.VMEM((16, 4, 2, 32, 512), BF16),
            pltpu.VMEM((8, 1024, 1024), BF16),
            pltpu.VMEM((256, 1024), F32),
            pltpu.SemaphoreType.DMA((10,)),
            pltpu.SemaphoreType.DMA((8,)),
        ],
        compiler_params=params,
        cost_estimate=cost(4_300_000_000, 30_000_000),
        name="outputs",
    )(pos, *x_pieces, dense)

    outputs, cm, cp = barrier((outputs, cm, cp))
    c2a, c2b = along_y(cm[:8], 1), along_y(cp[8:], -1)

    near = (class_rows, cm, cp)
    near = near + tuple(other_core(piece) for piece in near)
    cot_groups = cot_all.reshape(16, 8, 32, 1024)
    near_grad = pl.pallas_call(
        near_grad_kernel,
        in_specs=scalars[:1] + [anywhere] * 7,
        out_specs=anywhere,
        out_shape=jax.ShapeDtypeStruct((64, 8, 1024), F32),
        scratch_shapes=[
            pltpu.VMEM((6, 16, 32, 512), BF16),
            pltpu.VMEM((6, 16, 32, 1024), BF16),
            pltpu.VMEM((64, 8, 1024), F32),
            pltpu.SemaphoreType.DMA((6,)),
            pltpu.SemaphoreType.DMA((6,)),
            pltpu.SemaphoreType.DMA((1,)),
        ],
        compiler_params=params,
        cost_estimate=cost(3_200_000_000, 25_000_000),
        name="near_weight_grad",
    )(pos, *near, cot_groups)

    sum_m, sum_p, near_grad = barrier((sum_m, sum_p, near_grad))
    context_sum = (keep[0] + rest[0] + sum_m + sum_p).astype(BF16)
    context_grad = exchange(context_sum)

    weight_grad = pl.pallas_call(
        functools.partial(far_grad_kernel, 1.0 / math.sqrt(4096)),
        in_specs=scalars + [anywhere] * 6,
        out_shape=jax.ShapeDtypeStruct((1, 8, 34, 8, 128), BF16),
        scratch_shapes=[
            pltpu.VMEM((2, 16, 32, 512), BF16),
            pltpu.VMEM((2, 16, 32, 1024), BF16),
            pltpu.VMEM((64, 8, 1024), F32),
            pltpu.SemaphoreType.DMA((2, 2)),
            pltpu.SemaphoreType.DMA((2,)),
            pltpu.SemaphoreType.DMA((1,)),
        ],
        compiler_params=params,
        cost_estimate=cost(1_100_000_000, 18_000_000),
        name="far_weight_grad",
    )(*tables, c2a, c2b, other_core(c2a), other_core(c2b), cot_groups, near_grad)
    return (outputs, context_grad, weight_grad)


def solution(mesh):
    in_specs = (
        P(None, "mp", "seq"),
        P("mp", None, None, None, None),
        P(),
        P(),
        P(),
        P("seq", "mp"),
    )
    out_specs = (P("seq", "mp"), P(None, "mp", "seq"), P("mp", None, None, "seq", None))
    return jax.shard_map(
        on_device, mesh=mesh, in_specs=in_specs, out_specs=out_specs, check_vma=False
    )
```

```python
import functools
import math

import jax
import jax.numpy as jnp
from jax import lax
from jax.experimental import pallas as pl
from jax.experimental.pallas import tpu as pltpu
from jax.sharding import PartitionSpec as P

F32 = jnp.float32
BF16 = jnp.bfloat16
VMEM_LIMIT = 60 * 1024 * 1024


def build_panel(panel, blk_ref, rows_ref, cols_ref, live_ref, owner, j):
    panel[...] = jnp.zeros_like(panel)
    count = live_ref[owner, j]
    for k in range(34):
        r = pl.multiple_of((rows_ref[owner, j, k] - 8 * j) * 128, 128)
        c = pl.multiple_of((cols_ref[owner, j, k] - 8 * owner) * 128, 128)
        block = blk_ref[k]
        if k >= 30:
            block = jnp.where(k < count, block, jnp.zeros_like(block))
        panel[pl.ds(r, 128), pl.ds(c, 128)] = block


def start_all(copies):
    for copy in copies:
        copy.start()


def wait_all(copies):
    for copy in copies:
        copy.wait()


def transpose_kernel(x_ref, o_ref):
    x = x_ref[...].reshape(512, 512).astype(F32)
    t = x.T.reshape(4, 16, 8, 512)
    for part in range(16):
        o_ref[part] = t[:, part].reshape(32, 512).astype(BF16)


def partial_kernel(pos, rows, cols, live, cot, blk, keep, across, rest, dense, *scratch):
    lhs, keep_v, across_v, rest_v, cot_sem, blk_sem, out_sem = scratch[:7]
    blk_v, panels = scratch[7:15], scratch[15:23]
    owner = pos[0]
    y = owner // 2
    core = owner % 2
    cot_copies = []
    for d in range(4):
        for side in range(2):
            who = core if side == 0 else 1 - core
            cot_copies.append(
                pltpu.make_async_copy(
                    cot.at[(y + d) % 4, who], lhs.at[pl.ds(side * 128 + d * 32, 32)], cot_sem.at[side * 4 + d]
                )
            )
    blk_copies = [pltpu.make_async_copy(blk.at[0, j], blk_v[j], blk_sem.at[j]) for j in range(8)]
    start_all(cot_copies)
    start_all(blk_copies)

    out_copies = []
    blk_copies[0].wait()
    build_panel(panels[0], blk_v[0], rows, cols, live, owner, 0)
    wait_all(cot_copies)
    for j in range(8):
        if j < 7:
            blk_copies[j + 1].wait()
        res = lax.dot_general(lhs[...], panels[j][...], (((1,), (1,)), ((), ())), preferred_element_type=F32)
        if j < 7:
            build_panel(panels[j + 1], blk_v[j + 1], rows, cols, live, owner, j + 1)
        for half in range(2):
            lanes = slice(half * 512, half * 512 + 512)
            at = j * 2 + half
            for d in range(4):
                keep_v[d, at] = res[d * 32 : d * 32 + 32, lanes]
            rest_v[0, at] = res[128:160, lanes]
            rest_v[1, at] = res[160:192, lanes]
            across_v[at] = res[192:224, lanes]
            rest_v[2, at] = res[224:256, lanes]
        part = pl.ds(j * 2, 2)
        step_copies = [
            pltpu.make_async_copy(panels[j], dense.at[j], out_sem.at[j, 0]),
            pltpu.make_async_copy(keep_v.at[:, part], keep.at[:, part], out_sem.at[j, 1]),
            pltpu.make_async_copy(across_v.at[part], across.at[part], out_sem.at[j, 2]),
            pltpu.make_async_copy(rest_v.at[:, part], rest.at[:, part], out_sem.at[j, 3]),
        ]
        start_all(step_copies)
        out_copies += step_copies
    wait_all(out_copies)


def out_kernel(pos, a0, am, ap, a2a, a2b, b0, bm, bp, b2a, b2b, dense, out_ref, lhs, panels, acc, x_sem, dense_sem):
    owner = pos[0]
    y = owner // 2
    core = owner % 2
    x_copies = []
    for who, pieces in ((core, (a0, am, ap, a2a, a2b)), (1 - core, (b0, bm, bp, b2a, b2b))):
        places = (
            lhs.at[:, y, who],
            lhs.at[:, (y + 3) % 4, who],
            lhs.at[:, (y + 1) % 4, who],
            lhs.at[pl.ds(0, 8), (y + 2) % 4, who],
            lhs.at[pl.ds(8, 8), (y + 2) % 4, who],
        )
        for piece, place in zip(pieces, places):
            x_copies.append(pltpu.make_async_copy(piece, place, x_sem.at[len(x_copies)]))
    dense_copies = [pltpu.make_async_copy(dense.at[j], panels.at[j], dense_sem.at[j]) for j in range(8)]
    start_all(x_copies)
    start_all(dense_copies)
    wait_all(x_copies)
    for j in range(8):
        dense_copies[j].wait()
        first = jnp.dot(lhs[j * 2].reshape(256, 512), panels[j, :512], preferred_element_type=F32)
        second = jnp.dot(lhs[j * 2 + 1].reshape(256, 512), panels[j, 512:], preferred_element_type=F32)
        if j == 0:
            acc[...] = first + second
        elif j < 7:
            acc[...] += first + second
        else:
            out_ref[...] = (acc[...] + first + second).astype(BF16)


def token_group(owner, chip_step, core_step):
    return ((owner // 2 + chip_step) % 4) * 2 + (owner + core_step) % 2


def near_grad_kernel(pos, a0, am, ap, b0, bm, bp, g, total, x_v, g_v, acc, x_sem, g_sem, out_sem):
    owner = pos[0]
    copies = []
    for at, piece in enumerate((a0, am, ap, b0, bm, bp)):
        group = token_group(owner, (0, 3, 1)[at % 3], at // 3)
        copies.append(
            (
                pltpu.make_async_copy(piece, x_v.at[at], x_sem.at[at]),
                pltpu.make_async_copy(g.at[:, group], g_v.at[at], g_sem.at[at]),
            )
        )
        start_all(copies[-1])
    for at in range(6):
        wait_all(copies[at])
        x, cot = x_v[at].reshape(512, 512), g_v[at].reshape(512, 1024)
        res = jnp.dot(x, cot, preferred_element_type=F32).reshape(64, 8, 1024)
        if at == 0:
            acc[...] = res
        else:
            acc[...] += res
    out = pltpu.make_async_copy(acc, total, out_sem.at[0])
    out.start()
    out.wait()


def far_grad_kernel(scale, pos, rows, cols, live, a2a, a2b, b2a, b2b, g, near, out_ref, x_v, g_v, acc, x_sem, g_sem, near_sem):
    owner = pos[0]
    near_copy = pltpu.make_async_copy(near, acc, near_sem.at[0])
    near_copy.start()
    copies = []
    for at, (first, second) in enumerate(((a2a, a2b), (b2a, b2b))):
        group = token_group(owner, 2, at)
        copies.append(
            (
                pltpu.make_async_copy(first, x_v.at[at, pl.ds(0, 8)], x_sem.at[at, 0]),
                pltpu.make_async_copy(second, x_v.at[at, pl.ds(8, 8)], x_sem.at[at, 1]),
                pltpu.make_async_copy(g.at[:, group], g_v.at[at], g_sem.at[at]),
            )
        )
        start_all(copies[-1])
    near_copy.wait()
    for at in range(2):
        wait_all(copies[at])
        x, cot = x_v[at].reshape(512, 512), g_v[at].reshape(512, 1024)
        acc[...] += jnp.dot(x, cot, preferred_element_type=F32).reshape(64, 8, 1024)

    def pick(j, carry):
        count = live[owner, j]
        for k in range(34):
            r = rows[owner, j, k]
            c = pl.multiple_of((cols[owner, j, k] - 8 * owner) * 128, 128)
            tile = acc[r, :, pl.ds(c, 128)] * scale
            if k >= 30:
                tile = jnp.where(k < count, tile, 0.0)
            out_ref[0, j, k] = tile.astype(BF16)
        return carry

    lax.fori_loop(0, 8, pick, 0)


def on_device(context, blocks, row_blocks, col_blocks, live_counts, cotangent):
    owner = lax.axis_index("mp")
    pos = owner.astype(jnp.int32).reshape(1)
    tables = (pos, row_blocks, col_blocks, live_counts)
    params = pltpu.CompilerParams(vmem_limit_bytes=VMEM_LIMIT)
    barrier = lax.optimization_barrier

    def cost(flops, size):
        return pl.CostEstimate(flops=flops, bytes_accessed=size, transcendentals=0)

    def along_y(x, step):
        return lax.ppermute(x, "mp", [(i, (i + 2 * step) % 8) for i in range(8)])

    def other_core(x):
        return lax.ppermute(x, "mp", [(i, i ^ 1) for i in range(8)])

    def exchange(x):
        return lax.all_to_all(x, "seq", split_axis=0, concat_axis=0, tiled=True)

    cot_all = lax.all_gather(cotangent, "seq", axis=0, tiled=True)

    tokens = exchange(context)

    scalars = [pl.BlockSpec(memory_space=pltpu.SMEM)] * 4
    anywhere = pl.BlockSpec(memory_space=pl.ANY)
    keep, across, rest, dense = pl.pallas_call(
        partial_kernel,
        in_specs=scalars + [anywhere] * 2,
        out_specs=[anywhere] * 4,
        out_shape=[
            jax.ShapeDtypeStruct((4, 16, 32, 512), F32),
            jax.ShapeDtypeStruct((16, 32, 512), F32),
            jax.ShapeDtypeStruct((3, 16, 32, 512), F32),
            jax.ShapeDtypeStruct((8, 1024, 1024), BF16),
        ],
        scratch_shapes=[
            pltpu.VMEM((256, 1024), BF16),
            pltpu.VMEM((4, 16, 32, 512), F32),
            pltpu.VMEM((16, 32, 512), F32),
            pltpu.VMEM((3, 16, 32, 512), F32),
            pltpu.SemaphoreType.DMA((8,)),
            pltpu.SemaphoreType.DMA((8,)),
            pltpu.SemaphoreType.DMA((8, 4)),
        ]
        + [pltpu.VMEM((34, 128, 128), BF16)] * 8
        + [pltpu.VMEM((1024, 1024), BF16)] * 8,
        compiler_params=params,
        cost_estimate=cost(4_300_000_000, 45_000_000),
        name="partial_context_grad",
    )(*tables, cotangent.reshape(4, 2, 32, 1024), blocks)
    across, tokens = barrier((across, tokens))
    across = other_core(across)

    q2a, q2b = keep[2, :8] + across[:8], keep[2, 8:] + across[8:]
    q2a, q2b, tokens, rest, context = barrier((q2a, q2b, tokens, rest, context))
    from_a, from_b = along_y(q2a, 1), along_y(q2b, -1)
    xm, xp = along_y(tokens, 1), along_y(tokens, -1)
    rest = other_core(rest)

    by_class = pl.pallas_call(
        transpose_kernel,
        out_shape=jax.ShapeDtypeStruct((16, 32, 512), BF16),
        compiler_params=params,
        name="feature_rows",
    )(context)
    class_rows = exchange(by_class)

    x2a, x2b = along_y(xm[:8], 1), along_y(xp[8:], -1)
    x2a, x2b, class_rows = barrier((x2a, x2b, class_rows))
    own = (tokens, xm, xp, x2a, x2b)
    x_pieces = own + tuple(other_core(piece) for piece in own)

    cm, cp = along_y(class_rows, 1), along_y(class_rows, -1)

    q1 = jnp.concatenate([keep[1, :8] + rest[1, :8] + from_a, keep[1, 8:] + rest[1, 8:]], axis=0)
    q3 = jnp.concatenate([keep[3, :8] + rest[2, :8], keep[3, 8:] + rest[2, 8:] + from_b], axis=0)
    q1, q3, x_pieces = barrier((q1, q3, x_pieces))
    sum_m, sum_p = along_y(q1, 1), along_y(q3, -1)

    outputs = pl.pallas_call(
        out_kernel,
        in_specs=scalars[:1] + [anywhere] * 11,
        out_shape=jax.ShapeDtypeStruct((256, 1024), BF16),
        scratch_shapes=[
            pltpu.VMEM((16, 4, 2, 32, 512), BF16),
            pltpu.VMEM((8, 1024, 1024), BF16),
            pltpu.VMEM((256, 1024), F32),
            pltpu.SemaphoreType.DMA((10,)),
            pltpu.SemaphoreType.DMA((8,)),
        ],
        compiler_params=params,
        cost_estimate=cost(4_300_000_000, 30_000_000),
        name="outputs",
    )(pos, *x_pieces, dense)

    outputs, cm, cp = barrier((outputs, cm, cp))
    c2a, c2b = along_y(cm[:8], 1), along_y(cp[8:], -1)

    near = (class_rows, cm, cp)
    near = near + tuple(other_core(piece) for piece in near)
    cot_groups = cot_all.reshape(16, 8, 32, 1024)
    near_grad = pl.pallas_call(
        near_grad_kernel,
        in_specs=scalars[:1] + [anywhere] * 7,
        out_specs=anywhere,
        out_shape=jax.ShapeDtypeStruct((64, 8, 1024), F32),
        scratch_shapes=[
            pltpu.VMEM((6, 16, 32, 512), BF16),
            pltpu.VMEM((6, 16, 32, 1024), BF16),
            pltpu.VMEM((64, 8, 1024), F32),
            pltpu.SemaphoreType.DMA((6,)),
            pltpu.SemaphoreType.DMA((6,)),
            pltpu.SemaphoreType.DMA((1,)),
        ],
        compiler_params=params,
        cost_estimate=cost(3_200_000_000, 25_000_000),
        name="near_weight_grad",
    )(pos, *near, cot_groups)

    sum_m, sum_p, near_grad = barrier((sum_m, sum_p, near_grad))
    context_sum = (keep[0] + rest[0] + sum_m + sum_p).astype(BF16)
    context_grad = exchange(context_sum)

    weight_grad = pl.pallas_call(
        functools.partial(far_grad_kernel, 1.0 / math.sqrt(4096)),
        in_specs=scalars + [anywhere] * 6,
        out_shape=jax.ShapeDtypeStruct((1, 8, 34, 8, 128), BF16),
        scratch_shapes=[
            pltpu.VMEM((2, 16, 32, 512), BF16),
            pltpu.VMEM((2, 16, 32, 1024), BF16),
            pltpu.VMEM((64, 8, 1024), F32),
            pltpu.SemaphoreType.DMA((2, 2)),
            pltpu.SemaphoreType.DMA((2,)),
            pltpu.SemaphoreType.DMA((1,)),
        ],
        compiler_params=params,
        cost_estimate=cost(1_100_000_000, 18_000_000),
        name="far_weight_grad",
    )(*tables, c2a, c2b, other_core(c2a), other_core(c2b), cot_groups, near_grad)
    return (outputs, context_grad, weight_grad)


def solution(mesh):
    in_specs = (
        P(None, "mp", "seq"),
        P("mp", None, None, None, None),
        P(),
        P(),
        P(),
        P("seq", "mp"),
    )
    out_specs = (P("seq", "mp"), P(None, "mp", "seq"), P("mp", None, None, "seq", None))
    return jax.shard_map(
        on_device, mesh=mesh, in_specs=in_specs, out_specs=out_specs, check_vma=False
    )
```

```python
import functools
import math

import jax
import jax.numpy as jnp
from jax import lax
from jax.experimental import pallas as pl
from jax.experimental.pallas import tpu as pltpu
from jax.sharding import PartitionSpec as P

F32 = jnp.float32
BF16 = jnp.bfloat16
VMEM_LIMIT = 60 * 1024 * 1024


def build_panel(panel, blk_ref, rows_ref, cols_ref, live_ref, owner, j):
    panel[...] = jnp.zeros_like(panel)
    count = live_ref[owner, j]
    for k in range(34):
        r = pl.multiple_of((rows_ref[owner, j, k] - 8 * j) * 128, 128)
        c = pl.multiple_of((cols_ref[owner, j, k] - 8 * owner) * 128, 128)
        block = blk_ref[k]
        if k >= 30:
            block = jnp.where(k < count, block, jnp.zeros_like(block))
        panel[pl.ds(r, 128), pl.ds(c, 128)] = block


def start_all(copies):
    for copy in copies:
        copy.start()


def wait_all(copies):
    for copy in copies:
        copy.wait()


def transpose_kernel(x_ref, o_ref):
    x = x_ref[...].reshape(512, 512).astype(F32)
    t = x.T.reshape(4, 16, 8, 512)
    for part in range(16):
        o_ref[part] = t[:, part].reshape(32, 512).astype(BF16)


def partial_kernel(pos, rows, cols, live, cot, blk, keep, across, rest, dense, *scratch):
    lhs, keep_v, across_v, rest_v, cot_sem, blk_sem, out_sem = scratch[:7]
    blk_v, panels = scratch[7:15], scratch[15:23]
    owner = pos[0]
    y = owner // 2
    core = owner % 2
    cot_copies = []
    for d in range(4):
        for side in range(2):
            who = core if side == 0 else 1 - core
            cot_copies.append(
                pltpu.make_async_copy(
                    cot.at[(y + d) % 4, who], lhs.at[pl.ds(side * 128 + d * 32, 32)], cot_sem.at[side * 4 + d]
                )
            )
    blk_copies = [pltpu.make_async_copy(blk.at[0, j], blk_v[j], blk_sem.at[j]) for j in range(8)]
    start_all(cot_copies)
    start_all(blk_copies)

    out_copies = []
    blk_copies[0].wait()
    build_panel(panels[0], blk_v[0], rows, cols, live, owner, 0)
    wait_all(cot_copies)
    for j in range(8):
        if j < 7:
            blk_copies[j + 1].wait()
        res = lax.dot_general(lhs[...], panels[j][...], (((1,), (1,)), ((), ())), preferred_element_type=F32)
        if j < 7:
            build_panel(panels[j + 1], blk_v[j + 1], rows, cols, live, owner, j + 1)
        for half in range(2):
            lanes = slice(half * 512, half * 512 + 512)
            at = j * 2 + half
            for d in range(4):
                keep_v[d, at] = res[d * 32 : d * 32 + 32, lanes]
            rest_v[0, at] = res[128:160, lanes]
            rest_v[1, at] = res[160:192, lanes]
            across_v[at] = res[192:224, lanes]
            rest_v[2, at] = res[224:256, lanes]
        part = pl.ds(j * 2, 2)
        step_copies = [
            pltpu.make_async_copy(panels[j], dense.at[j], out_sem.at[j, 0]),
            pltpu.make_async_copy(keep_v.at[:, part], keep.at[:, part], out_sem.at[j, 1]),
            pltpu.make_async_copy(across_v.at[part], across.at[part], out_sem.at[j, 2]),
            pltpu.make_async_copy(rest_v.at[:, part], rest.at[:, part], out_sem.at[j, 3]),
        ]
        start_all(step_copies)
        out_copies += step_copies
    wait_all(out_copies)


def out_kernel(pos, a0, am, ap, a2a, a2b, b0, bm, bp, b2a, b2b, dense, out_ref, lhs, panels, acc, x_sem, dense_sem):
    owner = pos[0]
    y = owner // 2
    core = owner % 2
    x_copies = []
    for who, pieces in ((core, (a0, am, ap, a2a, a2b)), (1 - core, (b0, bm, bp, b2a, b2b))):
        places = (
            lhs.at[:, y, who],
            lhs.at[:, (y + 3) % 4, who],
            lhs.at[:, (y + 1) % 4, who],
            lhs.at[pl.ds(0, 8), (y + 2) % 4, who],
            lhs.at[pl.ds(8, 8), (y + 2) % 4, who],
        )
        for piece, place in zip(pieces, places):
            x_copies.append(pltpu.make_async_copy(piece, place, x_sem.at[len(x_copies)]))
    dense_copies = [pltpu.make_async_copy(dense.at[j], panels.at[j], dense_sem.at[j]) for j in range(8)]
    start_all(x_copies)
    start_all(dense_copies)
    wait_all(x_copies)
    for j in range(8):
        dense_copies[j].wait()
        first = jnp.dot(lhs[j * 2].reshape(256, 512), panels[j, :512], preferred_element_type=F32)
        second = jnp.dot(lhs[j * 2 + 1].reshape(256, 512), panels[j, 512:], preferred_element_type=F32)
        if j == 0:
            acc[...] = first + second
        elif j < 7:
            acc[...] += first + second
        else:
            out_ref[...] = (acc[...] + first + second).astype(BF16)


def token_group(owner, chip_step, core_step):
    return ((owner // 2 + chip_step) % 4) * 2 + (owner + core_step) % 2


def near_grad_kernel(pos, a0, am, ap, b0, bm, bp, g, total, x_v, g_v, acc, x_sem, g_sem, out_sem):
    owner = pos[0]
    copies = []
    for at, piece in enumerate((a0, am, ap, b0, bm, bp)):
        group = token_group(owner, (0, 3, 1)[at % 3], at // 3)
        copies.append(
            (
                pltpu.make_async_copy(piece, x_v.at[at], x_sem.at[at]),
                pltpu.make_async_copy(g.at[:, group], g_v.at[at], g_sem.at[at]),
            )
        )
        start_all(copies[-1])
    for at in range(6):
        wait_all(copies[at])
        x, cot = x_v[at].reshape(512, 512), g_v[at].reshape(512, 1024)
        res = jnp.dot(x, cot, preferred_element_type=F32).reshape(64, 8, 1024)
        if at == 0:
            acc[...] = res
        else:
            acc[...] += res
    out = pltpu.make_async_copy(acc, total, out_sem.at[0])
    out.start()
    out.wait()


def far_grad_kernel(scale, pos, rows, cols, live, a2a, a2b, b2a, b2b, g, near, out_ref, x_v, g_v, acc, x_sem, g_sem, near_sem):
    owner = pos[0]
    near_copy = pltpu.make_async_copy(near, acc, near_sem.at[0])
    near_copy.start()
    copies = []
    for at, (first, second) in enumerate(((a2a, a2b), (b2a, b2b))):
        group = token_group(owner, 2, at)
        copies.append(
            (
                pltpu.make_async_copy(first, x_v.at[at, pl.ds(0, 8)], x_sem.at[at, 0]),
                pltpu.make_async_copy(second, x_v.at[at, pl.ds(8, 8)], x_sem.at[at, 1]),
                pltpu.make_async_copy(g.at[:, group], g_v.at[at], g_sem.at[at]),
            )
        )
        start_all(copies[-1])
    near_copy.wait()
    for at in range(2):
        wait_all(copies[at])
        x, cot = x_v[at].reshape(512, 512), g_v[at].reshape(512, 1024)
        acc[...] += jnp.dot(x, cot, preferred_element_type=F32).reshape(64, 8, 1024)

    def pick(j, carry):
        count = live[owner, j]
        for k in range(34):
            r = rows[owner, j, k]
            c = pl.multiple_of((cols[owner, j, k] - 8 * owner) * 128, 128)
            tile = acc[r, :, pl.ds(c, 128)] * scale
            if k >= 30:
                tile = jnp.where(k < count, tile, 0.0)
            out_ref[0, j, k] = tile.astype(BF16)
        return carry

    lax.fori_loop(0, 8, pick, 0)


def on_device(context, blocks, row_blocks, col_blocks, live_counts, cotangent):
    owner = lax.axis_index("mp")
    pos = owner.astype(jnp.int32).reshape(1)
    tables = (pos, row_blocks, col_blocks, live_counts)
    params = pltpu.CompilerParams(vmem_limit_bytes=VMEM_LIMIT)
    barrier = lax.optimization_barrier

    def cost(flops, size):
        return pl.CostEstimate(flops=flops, bytes_accessed=size, transcendentals=0)

    def along_y(x, step):
        return lax.ppermute(x, "mp", [(i, (i + 2 * step) % 8) for i in range(8)])

    def other_core(x):
        return lax.ppermute(x, "mp", [(i, i ^ 1) for i in range(8)])

    def exchange(x):
        return lax.all_to_all(x, "seq", split_axis=0, concat_axis=0, tiled=True)

    cot_all = lax.all_gather(cotangent, "seq", axis=0, tiled=True)

    tokens = exchange(context)

    scalars = [pl.BlockSpec(memory_space=pltpu.SMEM)] * 4
    anywhere = pl.BlockSpec(memory_space=pl.ANY)
    keep, across, rest, dense = pl.pallas_call(
        partial_kernel,
        in_specs=scalars + [anywhere] * 2,
        out_specs=[anywhere] * 4,
        out_shape=[
            jax.ShapeDtypeStruct((4, 16, 32, 512), F32),
            jax.ShapeDtypeStruct((16, 32, 512), F32),
            jax.ShapeDtypeStruct((3, 16, 32, 512), F32),
            jax.ShapeDtypeStruct((8, 1024, 1024), BF16),
        ],
        scratch_shapes=[
            pltpu.VMEM((256, 1024), BF16),
            pltpu.VMEM((4, 16, 32, 512), F32),
            pltpu.VMEM((16, 32, 512), F32),
            pltpu.VMEM((3, 16, 32, 512), F32),
            pltpu.SemaphoreType.DMA((8,)),
            pltpu.SemaphoreType.DMA((8,)),
            pltpu.SemaphoreType.DMA((8, 4)),
        ]
        + [pltpu.VMEM((34, 128, 128), BF16)] * 8
        + [pltpu.VMEM((1024, 1024), BF16)] * 8,
        compiler_params=params,
        cost_estimate=cost(4_300_000_000, 45_000_000),
        name="partial_context_grad",
    )(*tables, cotangent.reshape(4, 2, 32, 1024), blocks)
    across, tokens = barrier((across, tokens))
    across = other_core(across)

    q2a, q2b = keep[2, :8] + across[:8], keep[2, 8:] + across[8:]
    q2a, q2b, tokens, rest, context = barrier((q2a, q2b, tokens, rest, context))
    from_a, from_b = along_y(q2a, 1), along_y(q2b, -1)
    xm, xp = along_y(tokens, 1), along_y(tokens, -1)
    rest = other_core(rest)

    by_class = pl.pallas_call(
        transpose_kernel,
        out_shape=jax.ShapeDtypeStruct((16, 32, 512), BF16),
        compiler_params=params,
        name="feature_rows",
    )(context)
    class_rows = exchange(by_class)

    x2a, x2b = along_y(xm[:8], 1), along_y(xp[8:], -1)
    x2a, x2b, class_rows = barrier((x2a, x2b, class_rows))
    own = (tokens, xm, xp, x2a, x2b)
    x_pieces = own + tuple(other_core(piece) for piece in own)

    cm, cp = along_y(class_rows, 1), along_y(class_rows, -1)

    p0, p1, p3 = barrier((keep[0] + rest[0], keep[1] + rest[1], keep[3] + rest[2]))
    q1 = jnp.concatenate([p1[:8] + from_a, p1[8:]], axis=0)
    q3 = jnp.concatenate([p3[:8], p3[8:] + from_b], axis=0)
    q1, q3, x_pieces = barrier((q1, q3, x_pieces))
    sum_m, sum_p = along_y(q1, 1), along_y(q3, -1)

    outputs = pl.pallas_call(
        out_kernel,
        in_specs=scalars[:1] + [anywhere] * 11,
        out_shape=jax.ShapeDtypeStruct((256, 1024), BF16),
        scratch_shapes=[
            pltpu.VMEM((16, 4, 2, 32, 512), BF16),
            pltpu.VMEM((8, 1024, 1024), BF16),
            pltpu.VMEM((256, 1024), F32),
            pltpu.SemaphoreType.DMA((10,)),
            pltpu.SemaphoreType.DMA((8,)),
        ],
        compiler_params=params,
        cost_estimate=cost(4_300_000_000, 30_000_000),
        name="outputs",
    )(pos, *x_pieces, dense)

    outputs, cm, cp = barrier((outputs, cm, cp))
    c2a, c2b = along_y(cm[:8], 1), along_y(cp[8:], -1)

    near = (class_rows, cm, cp)
    near = near + tuple(other_core(piece) for piece in near)
    cot_groups = cot_all.reshape(16, 8, 32, 1024)
    near_grad = pl.pallas_call(
        near_grad_kernel,
        in_specs=scalars[:1] + [anywhere] * 7,
        out_specs=anywhere,
        out_shape=jax.ShapeDtypeStruct((64, 8, 1024), F32),
        scratch_shapes=[
            pltpu.VMEM((6, 16, 32, 512), BF16),
            pltpu.VMEM((6, 16, 32, 1024), BF16),
            pltpu.VMEM((64, 8, 1024), F32),
            pltpu.SemaphoreType.DMA((6,)),
            pltpu.SemaphoreType.DMA((6,)),
            pltpu.SemaphoreType.DMA((1,)),
        ],
        compiler_params=params,
        cost_estimate=cost(3_200_000_000, 25_000_000),
        name="near_weight_grad",
    )(pos, *near, cot_groups)

    sum_m, sum_p, near_grad = barrier((sum_m, sum_p, near_grad))
    context_sum = (p0 + sum_m + sum_p).astype(BF16)
    context_grad = exchange(context_sum)

    weight_grad = pl.pallas_call(
        functools.partial(far_grad_kernel, 1.0 / math.sqrt(4096)),
        in_specs=scalars + [anywhere] * 6,
        out_shape=jax.ShapeDtypeStruct((1, 8, 34, 8, 128), BF16),
        scratch_shapes=[
            pltpu.VMEM((2, 16, 32, 512), BF16),
            pltpu.VMEM((2, 16, 32, 1024), BF16),
            pltpu.VMEM((64, 8, 1024), F32),
            pltpu.SemaphoreType.DMA((2, 2)),
            pltpu.SemaphoreType.DMA((2,)),
            pltpu.SemaphoreType.DMA((1,)),
        ],
        compiler_params=params,
        cost_estimate=cost(1_100_000_000, 18_000_000),
        name="far_weight_grad",
    )(*tables, c2a, c2b, other_core(c2a), other_core(c2b), cot_groups, near_grad)
    return (outputs, context_grad, weight_grad)


def solution(mesh):
    in_specs = (
        P(None, "mp", "seq"),
        P("mp", None, None, None, None),
        P(),
        P(),
        P(),
        P("seq", "mp"),
    )
    out_specs = (P("seq", "mp"), P(None, "mp", "seq"), P("mp", None, None, "seq", None))
    return jax.shard_map(
        on_device, mesh=mesh, in_specs=in_specs, out_specs=out_specs, check_vma=False
    )
```
